256 devices in a mesh: section: 4 (over x), vocab: 64 (over z, y, core).
Axes of the slice: x: 4, y: 4, z: 8, core: 2. Of those that a mesh axis runs over, the one named last changes fastest.
Arguments:
- hidden: bfloat16 [4, 128, 8192], P('section', 'vocab'), may hold values from -240 to 240
- out_head: bfloat16 [8192, 65536], P('section', 'vocab'), may hold values from -1 to 1
- targets: int32 [4, 128], P('section'), may hold values from 0 to 65535
- scale_index: int32 [4], P('section'), may hold values from 0 to 7
Outputs:
- grad_head: bfloat16 [8192, 65536], P('section', 'vocab')
- grad_hidden: bfloat16 [4, 128, 8192], P('section', 'vocab')
- exit_loss: float32 [4], P('section')
The draws below stay inside these ranges and needn't reach their ends.
All inputs are finite; a program needn't handle non-finite values.
Results may differ from the reference program's by a relative error of at most 0.0055.
Values may be sent and summed in bfloat16 or wider, within the bound.
A program may use at most 64 MiB of HBM per device.

```python
import math
import jax
import jax.numpy as jnp
import numpy as np

D = 8192
ROWS = 128
SECTIONS = 4
VOCAB = 65536


def shared_head(key, common):
    column_key, common_key = jax.random.split(key)
    values = jnp.clip(jax.random.normal(column_key, (D, VOCAB), jnp.float32), -5.0, 5.0) / math.sqrt(D)
    shared = common * jnp.clip(jax.random.normal(common_key, (D, 1), jnp.float32), -4.0, 4.0) / math.sqrt(D)
    return values + shared


def draw_out_head(key, part):
    weights = shared_head(key, 0.5)
    return weights.astype(jnp.bfloat16)


def draw_hidden(key, part):
    key = jax.random.fold_in(key, 11)
    first_key = jax.random.fold_in(key, 0)
    values = 3.0 * jnp.clip(jax.random.normal(first_key, (SECTIONS, ROWS, D), jnp.float32), -5.0, 5.0)
    return values.astype(jnp.bfloat16)


def set_ends(result, own_key, low, high):
    spot = [jax.random.randint(jax.random.fold_in(own_key, axis), (), 0, length) for axis, length in enumerate(result.shape)]
    widest = result.shape.index(max(result.shape))
    beside = spot[:widest] + [(spot[widest] + 1) % result.shape[widest]] + spot[widest + 1:]
    return result.at[tuple(spot)].set(low).at[tuple(beside)].set(high)


def rank_table(amount, lean):
    loads = [(1 << 20) // math.isqrt(grade ** lean) + 1 for grade in range(1, amount + 1)]
    deviation = 1 + sum(loads) // (1 << 30)
    return np.cumsum(np.array([max(1, weight // deviation) for weight in loads]))


def ranked_ids(own_key, shape, amount, lean):
    table = rank_table(amount, lean)
    ticket = jax.random.randint(jax.random.fold_in(own_key, 1), shape, 0, int(table[amount - 1]))
    grade = jnp.searchsorted(jnp.asarray(table, jnp.int32), ticket, side="right")
    return jax.random.permutation(jax.random.fold_in(own_key, 2), amount)[grade].astype(jnp.int32)


def setup_inputs(seed: int = 0) -> dict:
    splits = jax.random.split(jax.random.key(seed), 5)
    hidden = draw_hidden(jax.random.fold_in(splits[4], 71), 0)
    out_head = draw_out_head(jax.random.fold_in(splits[4], 71), 0)
    targets = set_ends(ranked_ids(splits[2], (SECTIONS, ROWS), VOCAB, 2), jax.random.fold_in(splits[2], 3), 0, VOCAB - 1).astype(jnp.int32)
    scale_index = set_ends(jax.random.randint(splits[3], (SECTIONS,), 0, 8), jax.random.fold_in(splits[3], 1), 0, 7).astype(jnp.int32)
    return {"hidden": hidden, "out_head": out_head, "targets": targets, "scale_index": scale_index}


def reference(hidden, out_head, targets, scale_index):
    losses = []
    grads = []
    exit_grads = []
    columns = jnp.arange(VOCAB, dtype=jnp.int32)
    for section in range(SECTIONS):
        logits = jnp.dot(hidden[section], out_head, preferred_element_type=jnp.float32)
        peak = jnp.max(logits, axis=1)
        total = jnp.sum(jnp.exp(logits - peak[:, None]), axis=1)
        lse = peak + jnp.log(total)
        onehot = (targets[section][:, None] == columns[None, :]).astype(jnp.float32)
        target_logit = jnp.sum(logits * onehot, axis=1)
        losses.append(jnp.mean(lse - target_logit))
        weight = 4.0 * (scale_index[section].astype(jnp.float32) + 1.0)
        exit_grad = (weight * (jnp.exp(logits - lse[:, None]) - onehot)).astype(jnp.bfloat16)
        exit_grads.append(exit_grad)
        grads.append(jnp.dot(exit_grad, out_head.T, preferred_element_type=jnp.float32).astype(jnp.bfloat16))
    every_grad = jnp.concatenate(exit_grads, axis=0)
    every_hidden = hidden.reshape(SECTIONS * ROWS, D)
    grad_head = jnp.dot(every_hidden.T, every_grad, preferred_element_type=jnp.float32).astype(jnp.bfloat16)
    return grad_head, jnp.stack(grads), jnp.stack(losses)
```

```python
import functools

import jax
import jax.numpy as jnp
from jax import lax
from jax.experimental import pallas as pl
from jax.experimental.pallas import tpu as pltpu
from jax.sharding import PartitionSpec as P

MESH = pl.DeviceIdType.MESH
F32 = jnp.float32
BF16 = jnp.bfloat16

NX, NZ, NY = 4, 8, 4
LANES = 128
SUB = 16
FEAT = SUB * LANES
WIDTH = 1024
HALF = WIDTH // 2
GROUP = NY * NZ
CHUNK = NX * GROUP


def kernel(
    hid, w_hbm, tgt, scale, head_hbm, ghid, loss,
    w, head, hs32, hs, g, f, h, part, relay, final, u, grad,
    st_send, st_core, st_y, st_z, st_x,
    core_out, core_in, keep, y_out, y_in, zf, z_out, z_in, x_out, x_in,
    w_sem, head_sem,
    hx_s, hx_r, hz_s, hz_r, hy_s, hy_r, hc_s, hc_r,
    rl_s, rl_r, fn_s, fn_r, ux_s, ux_r,
    sc_s, sc_r, sy_s, sy_r, sz_s, sz_r, sx_s, sx_r,
    gc_s, gc_r, gy_s, gy_r, gz_s, gz_r, gx_s, gx_r,
):
    x = lax.axis_index("section")
    v = lax.axis_index("vocab")
    z, y, c = v // 8, (v // 2) % 4, v % 2
    oc = 1 - c

    def at(px, pz, py, pc):
        return (px, (pz * NY + py) * 2 + pc)

    def x_peer(d):
        return at((x + d) % NX, z, y, c)

    def y_peer(d):
        return at(x, z, (y + d) % NY, c)

    def z_peer(d):
        return at(x, (z + d) % NZ, y, c)

    core_peer = at(x, z, y, oc)
    sent = []

    def send(src, dst, s_sem, r_sem, peer):
        copy = pltpu.make_async_remote_copy(
            src_ref=src, dst_ref=dst, send_sem=s_sem, recv_sem=r_sem,
            device_id=peer, device_id_type=MESH,
        )
        copy.start()
        sent.append(copy)

    def got(ref, sem):
        pltpu.make_async_copy(ref, ref, sem).wait()

    barrier = pltpu.get_barrier_semaphore()
    peers = (
        [x_peer(d) for d in range(1, NX)]
        + [core_peer]
        + [y_peer(d) for d in range(1, NY)]
        + [z_peer(d) for d in range(1, NZ)]
    )
    for peer in peers:
        pl.semaphore_signal(barrier, inc=1, device_id=peer, device_id_type=MESH)

    w_copy = pltpu.make_async_copy(w_hbm, w, w_sem)
    w_copy.start()

    own = hid[0].astype(F32)
    for xx in range(NX):
        for k in range(SUB):
            at0 = xx * FEAT + k * LANES
            hs32[xx, :, k, :] = own[:, at0 : at0 + LANES]
    hs[...] = hs32[...].astype(BF16)

    place = lax.broadcasted_iota(jnp.int32, (128, 128), 0)
    row = lax.broadcasted_iota(jnp.int32, (128, 128), 1)
    pl_l, pl_c, pl_y, pl_z = place // 64, (place // 32) % 2, (place // 8) % 4, place % 8
    match = row == pl_z * 16 + pl_y * 4 + pl_c * 2 + pl_l
    tcol_all = jnp.sum(
        jnp.where(match, tgt[...].astype(F32), 0.0), axis=1, keepdims=True
    )
    eye = place == row
    trow_all = jnp.sum(jnp.where(eye, tcol_all, 0.0), axis=0, keepdims=True)
    st_x[x, 2:3, :] = trow_all
    st_send[0] = jnp.zeros((8, LANES), F32)

    pl.semaphore_wait(barrier, len(peers))

    for d in range(1, NX):
        send(hs.at[(x + d) % NX], g.at[:, c, x, y, z], hx_s.at[d - 1], hx_r.at[d - 1], x_peer(d))
    for l in range(2):
        g[l, c, x, y, z] = hs[x, l]
    for d in range(1, NX):
        got(hs.at[0], hx_r.at[d - 1])

    for l in range(2):
        for d in range(1, NZ):
            piece = g.at[l, c, :, y, z]
            send(piece, piece, hz_s.at[l, d - 1], hz_r.at[l, d - 1], z_peer(d))
    for l in range(2):
        for d in range(1, NZ):
            got(g.at[l, c, :, y, 0], hz_r.at[l, d - 1])
        block = g.at[l, c, :, y]
        for d in range(1, NY):
            send(block, block, hy_s.at[l, d - 1], hy_r.at[l, d - 1], y_peer(d))
        send(block, block, hc_s.at[l, 0], hc_r.at[l, 0], core_peer)

    def gathered_own(l):
        for d in range(1, NY):
            block = g.at[l, c, :, (y + NY - d) % NY]
            got(block, hy_r.at[l, d - 1])
            send(block, block, hc_s.at[l, d], hc_r.at[l, d], core_peer)

    def gathered_other(l):
        for d in range(NY):
            got(g.at[l, oc, :, 0], hc_r.at[l, d])

    def logits_part(l, cc, k):
        f[...] = g[l, cc].reshape(CHUNK * SUB, LANES).astype(F32)
        for j in range(SUB):
            h[l, cc, :, j * LANES : (j + 1) * LANES] = f[pl.ds(j, CHUNK, stride=SUB), :].astype(BF16)
        if k == 0:
            w_copy.wait()

        def tile(n, _):
            cols = pl.ds(pl.multiple_of(n * 256, 256), 256)
            out = jnp.dot(h[l, cc], w[:, cols], preferred_element_type=F32)
            part[k, :, :, cols] = out.reshape(NX, GROUP, 256)
            return 0

        lax.fori_loop(0, WIDTH // 256, tile, 0)
        far = part.at[k, (x + 2) % NX]
        send(far.at[:, pl.ds(0, HALF)], relay.at[k, 0], rl_s.at[k, 0], rl_r.at[k, 0], x_peer(1))
        send(far.at[:, pl.ds(HALF, HALF)], relay.at[k, 1], rl_s.at[k, 1], rl_r.at[k, 1], x_peer(3))

    def logits_relay(k):
        right, left = (x + 1) % NX, (x + 3) % NX
        got(relay.at[k, 0], rl_r.at[k, 0])
        part[k, right, :, :HALF] = part[k, right, :, :HALF] + relay[k, 0]
        send(part.at[k, right], final.at[k, 0], fn_s.at[k, 0], fn_r.at[k, 0], x_peer(1))
        got(relay.at[k, 1], rl_r.at[k, 1])
        part[k, left, :, HALF:] = part[k, left, :, HALF:] + relay[k, 1]
        send(part.at[k, left], final.at[k, 1], fn_s.at[k, 1], fn_r.at[k, 1], x_peer(3))

    columns = v * WIDTH + lax.broadcasted_iota(jnp.int32, (GROUP, WIDTH), 1)
    lane = lax.broadcasted_iota(jnp.int32, (GROUP, LANES), 1)
    sub = lax.broadcasted_iota(jnp.int32, (GROUP, LANES), 0)

    def first_lane(l, cc):
        return (l * 2 + cc) * GROUP

    def as_column(line, l, cc):
        here = lane == sub + first_lane(l, cc)
        return jnp.sum(jnp.where(here, line, 0.0), axis=1, keepdims=True)

    def softmax_part(l, cc, k):
        got(final.at[k, 0], fn_r.at[k, 0])
        got(final.at[k, 1], fn_r.at[k, 1])
        logits = part[k, x] + final[k, 0] + final[k, 1]
        peak = jnp.max(logits, axis=1, keepdims=True)
        raised = jnp.exp(logits - peak)
        total = jnp.sum(raised, axis=1, keepdims=True)
        target = as_column(trow_all, l, cc).astype(jnp.int32)
        hit = jnp.sum(jnp.where(columns == target, logits, 0.0), axis=1, keepdims=True)
        u[l, cc, x] = raised.astype(BF16)
        for d in range(1, NX):
            send(u.at[l, cc, x], u.at[l, cc, x], ux_s.at[k, d - 1], ux_r.at[k, d - 1], x_peer(d))
        here = lane == sub + first_lane(l, cc)
        for i, value in enumerate((peak, total, hit)):
            line = jnp.sum(jnp.where(here, value, 0.0), axis=0, keepdims=True)
            st_send[0, i : i + 1, :] = st_send[0, i : i + 1, :] + line

    order = [(0, c), (0, oc), (1, c), (1, oc)]
    gathered_own(0)
    logits_part(0, c, 0)
    gathered_other(0)
    logits_part(0, oc, 1)
    logits_relay(0)
    logits_relay(1)
    gathered_own(1)
    logits_part(1, c, 2)
    gathered_other(1)
    logits_part(1, oc, 3)
    softmax_part(0, c, 0)
    softmax_part(0, oc, 1)
    logits_relay(2)
    logits_relay(3)
    softmax_part(1, c, 2)
    softmax_part(1, oc, 3)

    def merged(parts):
        peak = functools.reduce(jnp.maximum, [p[0:1] for p in parts])
        total = functools.reduce(jnp.add, [p[1:2] * jnp.exp(p[0:1] - peak) for p in parts])
        hit = functools.reduce(jnp.add, [p[2:3] for p in parts])
        return peak, total, hit

    def put(ref, values):
        for i, value in enumerate(values):
            ref[i : i + 1, :] = value

    send(st_send.at[0], st_core, sc_s, sc_r, core_peer)
    got(st_core, sc_r)
    put(st_send.at[1], merged([st_send[0], st_core[...]]))
    st_y[y] = st_send[1]
    for d in range(1, NY):
        send(st_send.at[1], st_y.at[y], sy_s.at[d - 1], sy_r.at[d - 1], y_peer(d))
    for d in range(1, NY):
        got(st_core, sy_r.at[d - 1])
    put(st_send.at[2], merged([st_y[i] for i in range(NY)]))
    st_z[z] = st_send[2]
    for d in range(1, NZ):
        send(st_send.at[2], st_z.at[z], sz_s.at[d - 1], sz_r.at[d - 1], z_peer(d))
    for d in range(1, NZ):
        got(st_core, sz_r.at[d - 1])
    peak, total, hit = merged([st_z[i] for i in range(NZ)])
    lse = peak + jnp.log(total)
    loss[...] = jnp.sum(lse - hit, axis=1, keepdims=True) * (1.0 / 128.0)
    weight = 4.0 * (jnp.full((1, LANES), scale[0], jnp.int32).astype(F32) + 1.0)
    st_x[x, 0:1, :] = weight * jnp.exp(st_send[0, 0:1, :] - lse)
    st_x[x, 1:2, :] = weight * (jnp.exp(hit - lse) - 1.0)
    for d in range(1, NX):
        send(st_x.at[x], st_x.at[x], sx_s.at[d - 1], sx_r.at[d - 1], x_peer(d))
    for k in range(4):
        for d in range(1, NX):
            got(u.at[0, 0, 0], ux_r.at[k, d - 1])
    for d in range(1, NX):
        got(st_core, sx_r.at[d - 1])

    def gradient(l, cc):
        for s in range(NX):
            factor = as_column(st_x[s, 0:1, :], l, cc)
            entry = as_column(st_x[s, 1:2, :], l, cc)
            target = as_column(st_x[s, 2:3, :], l, cc).astype(jnp.int32)
            value = jnp.where(columns == target, entry, u[l, cc, s].astype(F32) * factor)
            grad[l, cc, s * GROUP : (s + 1) * GROUP, :] = value.astype(BF16)

    def hidden_part(l, cc, out, kind):
        def tile(n, _):
            rows = pl.ds(pl.multiple_of(n * 256, 256), 256)
            value = lax.dot_general(
                grad[l, cc], w[rows, :], (((1,), (1,)), ((), ())), preferred_element_type=F32
            )
            out[l, :, rows] = value.astype(kind)
            return 0

        lax.fori_loop(0, FEAT // 256, tile, 0)

    for l in range(2):
        gradient(l, oc)
        hidden_part(l, oc, core_out, BF16)
        send(core_out.at[l], core_in.at[l], gc_s.at[l], gc_r.at[l], core_peer)
        gradient(l, c)
        hidden_part(l, c, keep, F32)

    for l in range(2):
        got(core_in.at[l], gc_r.at[l])
        keep[l] = keep[l] + core_in[l].astype(F32)
        for d in range(1, NY):
            py = (y + d) % NY
            for s in range(NX):
                rows = pl.ds(pl.multiple_of(s * GROUP + py * NZ, NZ), NZ)
                zf[pl.ds(s * NZ, NZ), :] = keep[l, rows, :]
            y_out[l, d - 1] = zf[...].astype(BF16)
            send(y_out.at[l, d - 1], y_in.at[l, d - 1], gy_s.at[l, d - 1], gy_r.at[l, d - 1], y_peer(d))

    def head_tile(n, _):
        rows = pl.ds(pl.multiple_of(n * 256, 256), 256)
        out = jnp.zeros((256, WIDTH), F32)
        for l in range(2):
            for cc in range(2):
                out = out + lax.dot_general(
                    h[l, cc, :, rows], grad[l, cc], (((0,), (0,)), ((), ())), preferred_element_type=F32
                )
        head[rows, :] = out.astype(BF16)
        return 0

    lax.fori_loop(0, FEAT // 256, head_tile, 0)
    head_copy = pltpu.make_async_copy(head, head_hbm, head_sem)
    head_copy.start()

    for l in range(2):
        for d in range(1, NY):
            got(y_in.at[l, d - 1], gy_r.at[l, d - 1])
        for s in range(NX):
            rows = pl.ds(pl.multiple_of(s * GROUP + y * NZ, NZ), NZ)
            zf[pl.ds(s * NZ, NZ), :] = keep[l, rows, :]
        acc = zf[...]
        for d in range(1, NY):
            acc = acc + y_in[l, d - 1].astype(F32)
        for j in range(SUB):
            f[pl.ds(j, NX * NZ, stride=SUB), :] = acc[:, j * LANES : (j + 1) * LANES]
        z_out[l] = f[: NX * NZ * SUB, :].reshape(NX, NZ, SUB, LANES).astype(BF16)
        z_in[l, z] = z_out[l, :, z]
        for d in range(1, NZ):
            send(z_out.at[l, :, (z + d) % NZ], z_in.at[l, z], gz_s.at[l, d - 1], gz_r.at[l, d - 1], z_peer(d))
    for l in range(2):
        for d in range(1, NZ):
            got(z_in.at[l, 0], gz_r.at[l, d - 1])
        acc = z_in[l, 0].astype(F32)
        for i in range(1, NZ):
            acc = acc + z_in[l, i].astype(F32)
        x_out[:, l] = acc.astype(BF16)
    x_in[x] = x_out[x]
    for d in range(1, NX):
        send(x_out.at[(x + d) % NX], x_in.at[x], gx_s.at[d - 1], gx_r.at[d - 1], x_peer(d))
    for d in range(1, NX):
        got(x_in.at[0], gx_r.at[d - 1])
    hs32[...] = x_in[...].astype(F32)
    for xx in range(NX):
        for k in range(SUB):
            at0 = xx * FEAT + k * LANES
            ghid[0, :, at0 : at0 + LANES] = hs32[xx, :, k, :].astype(BF16)
    for copy in sent:
        copy.wait_send()
    head_copy.wait()


def on_device(hidden, out_head, targets, scale_index):
    vmem = pltpu.VMEM
    dma = pltpu.SemaphoreType.DMA
    scratch = [
        vmem((FEAT, WIDTH), BF16),
        vmem((FEAT, WIDTH), BF16),
        vmem((NX, 2, SUB, LANES), F32),
        vmem((NX, 2, SUB, LANES), BF16),
        vmem((2, 2, NX, NY, NZ, SUB, LANES), BF16),
        vmem((CHUNK * SUB, LANES), F32),
        vmem((2, 2, CHUNK, FEAT), BF16),
        vmem((4, NX, GROUP, WIDTH), F32),
        vmem((4, 2, GROUP, HALF), F32),
        vmem((4, 2, GROUP, WIDTH), F32),
        vmem((2, 2, NX, GROUP, WIDTH), BF16),
        vmem((2, 2, CHUNK, WIDTH), BF16),
        vmem((3, 8, LANES), F32),
        vmem((8, LANES), F32),
        vmem((NY, 8, LANES), F32),
        vmem((NZ, 8, LANES), F32),
        vmem((NX, 8, LANES), F32),
        vmem((2, CHUNK, FEAT), BF16),
        vmem((2, CHUNK, FEAT), BF16),
        vmem((2, CHUNK, FEAT), F32),
        vmem((2, NY - 1, NX * NZ, FEAT), BF16),
        vmem((2, NY - 1, NX * NZ, FEAT), BF16),
        vmem((NX * NZ, FEAT), F32),
        vmem((2, NX, NZ, SUB, LANES), BF16),
        vmem((2, NZ, NX, SUB, LANES), BF16),
        vmem((NX, 2, SUB, LANES), BF16),
        vmem((NX, 2, SUB, LANES), BF16),
        dma, dma,
        dma((3,)), dma((3,)), dma((2, 7)), dma((2, 7)),
        dma((2, 3)), dma((2, 3)), dma((2, 4)), dma((2, 4)),
        dma((4, 2)), dma((4, 2)), dma((4, 2)), dma((4, 2)), dma((4, 3)), dma((4, 3)),
        dma, dma, dma((3,)), dma((3,)), dma((7,)), dma((7,)), dma((3,)), dma((3,)),
        dma((2,)), dma((2,)), dma((2, 3)), dma((2, 3)),
        dma((2, 7)), dma((2, 7)), dma((3,)), dma((3,)),
    ]
    in_vmem = pl.BlockSpec(memory_space=pltpu.VMEM)
    head, ghid, loss = pl.pallas_call(
        kernel,
        out_shape=(
            jax.ShapeDtypeStruct((FEAT, WIDTH), BF16),
            jax.ShapeDtypeStruct(hidden.shape, BF16),
            jax.ShapeDtypeStruct((1, 1), F32),
        ),
        in_specs=[
            in_vmem,
            pl.BlockSpec(memory_space=pl.ANY),
            in_vmem,
            pl.BlockSpec(memory_space=pltpu.SMEM),
        ],
        out_specs=(pl.BlockSpec(memory_space=pl.ANY), in_vmem, in_vmem),
        scratch_shapes=scratch,
        compiler_params=pltpu.CompilerParams(
            collective_id=0, has_side_effects=True, vmem_limit_bytes=56 * 2**20
        ),
    )(hidden, out_head, targets, scale_index)
    return head, ghid, loss.reshape(1)


def solution(mesh):
    in_specs = (
        P("section", "vocab", None),
        P("section", "vocab"),
        P("section", None),
        P("section"),
    )
    out_specs = (P("section", "vocab"), P("section", "vocab", None), P("section"))
    return jax.shard_map(
        on_device, mesh=mesh, in_specs=in_specs, out_specs=out_specs, check_vma=False
    )
```

```python
import functools

import jax
import jax.numpy as jnp
from jax import lax
from jax.experimental import pallas as pl
from jax.experimental.pallas import tpu as pltpu
from jax.sharding import PartitionSpec as P

MESH = pl.DeviceIdType.MESH
F32 = jnp.float32
BF16 = jnp.bfloat16

NX, NZ, NY = 4, 8, 4
LANES = 128
SUB = 16
FEAT = SUB * LANES
WIDTH = 1024
HALF = WIDTH // 2
GROUP = NY * NZ
CHUNK = NX * GROUP
VMEM_MIB = 46


def kernel(
    hid, w_hbm, tgt, scale, head, ghid, loss,
    w, wt, hs32, hs, g, f, h, part, relay, final, u, grad, hot, hot_w, raw,
    tx, st_send, st_core, st_y, st_z, st_x,
    core_out, core_in, keep, y_out, y_in, zf, z_out, z_in, x_out, x_in,
    w_sem, hx_r, tx_r, hz_r, hy_r, hc_r, rl_r, fn_r, ux_r,
    sc_r, sy_r, sz_r, sx_r, gc_r, gy_r, gz_r, gx_r,
    hx_s, tx_s, hz_s, hy_s, hc_s, rl_s, fn_s, ux_s,
    sc_s, sy_s, sz_s, sx_s, gc_s, gy_s, gz_s, gx_s,
):
    x = lax.axis_index("section")
    v = lax.axis_index("vocab")
    z, y, c = v // 8, (v // 2) % 4, v % 2
    oc = 1 - c

    def at(px, pz, py, pc):
        return (px, (pz * NY + py) * 2 + pc)

    def x_peer(d):
        return at((x + d) % NX, z, y, c)

    def y_peer(d):
        return at(x, z, (y + d) % NY, c)

    def z_peer(d):
        return at(x, (z + d) % NZ, y, c)

    core_peer = at(x, z, y, oc)

    def send(src, dst, s_sem, r_sem, peer):
        pltpu.make_async_remote_copy(
            src_ref=src, dst_ref=dst, send_sem=s_sem, recv_sem=r_sem,
            device_id=peer, device_id_type=MESH,
        ).start()

    def got(ref, sem):
        pltpu.make_async_copy(ref, ref, sem).wait()

    barrier = pltpu.get_barrier_semaphore()
    peers = (
        [x_peer(d) for d in range(1, NX)]
        + [core_peer]
        + [y_peer(d) for d in range(1, NY)]
        + [z_peer(d) for d in range(1, NZ)]
    )
    for peer in peers:
        pl.semaphore_signal(barrier, inc=1, device_id=peer, device_id_type=MESH)

    w_copy = pltpu.make_async_copy(w_hbm, w, w_sem)
    w_copy.start()

    own = hid[0].astype(F32)
    for xx in range(NX):
        for k in range(SUB):
            at0 = xx * FEAT + k * LANES
            hs32[xx, :, k, :] = own[:, at0 : at0 + LANES]
    hs[...] = hs32[...].astype(BF16)

    place = lax.broadcasted_iota(jnp.int32, (128, 128), 0)
    row = lax.broadcasted_iota(jnp.int32, (128, 128), 1)
    pl_l, pl_c, pl_y, pl_z = place // 64, (place // 32) % 2, (place // 8) % 4, place % 8
    match = row == pl_z * 16 + pl_y * 4 + pl_c * 2 + pl_l
    tcol_all = jnp.sum(
        jnp.where(match, tgt[...].astype(F32), 0.0), axis=1, keepdims=True
    )
    tx[x] = jnp.broadcast_to(
        jnp.sum(jnp.where(place == row, tcol_all, 0.0), axis=0, keepdims=True), (8, LANES)
    )
    st_send[...] = jnp.zeros_like(st_send)
    st_x[...] = jnp.zeros_like(st_x)

    pl.semaphore_wait(barrier, len(peers))

    for d in range(1, NX):
        send(hs.at[(x + d) % NX], g.at[:, c, x, y, z], hx_s, hx_r, x_peer(d))
    for d in range(1, NX):
        send(tx.at[x], tx.at[x], tx_s, tx_r, x_peer(d))
    for l in range(2):
        g[l, c, x, y, z] = hs[x, l]
    got(hs.at[pl.ds(0, 3)], hx_r)

    for l in range(2):
        for d in range(1, NZ):
            piece = g.at[l, c, :, y, z]
            send(piece, piece, hz_s, hz_r.at[l], z_peer(d))

    columns = v * WIDTH + lax.broadcasted_iota(jnp.int32, (GROUP, WIDTH), 1)
    lane = lax.broadcasted_iota(jnp.int32, (GROUP, LANES), 1)
    sub = lax.broadcasted_iota(jnp.int32, (GROUP, LANES), 0)

    def spot(l, cc):
        return lane == sub + (l * 2 + cc) * GROUP

    def as_column(line, l, cc):
        return jnp.sum(jnp.where(spot(l, cc), line, 0.0), axis=1, keepdims=True)

    def target_column(s, l, cc):
        return as_column(tx[s, 0:1, :], l, cc).astype(jnp.int32)

    def rows_of(l, cc):
        return pl.ds(pl.multiple_of((l * 2 + cc) * CHUNK, CHUNK), CHUNK)

    got(tx.at[pl.ds(0, 3)], tx_r)
    w_copy.wait()

    def turn(n, _):
        rows = pl.ds(pl.multiple_of(n * 512, 512), 512)
        wt[:, rows] = w[rows, :].T
        return 0

    lax.fori_loop(0, FEAT // 512, turn, 0)

    def target_rows(l, cc):
        for s in range(NX):
            here = columns == target_column(s, l, cc)
            hot[s * GROUP : (s + 1) * GROUP, :] = jnp.where(here, 1.0, 0.0).astype(BF16)
        hot_w[l, cc] = jnp.dot(hot[...], wt[...], preferred_element_type=F32).astype(BF16)

    target_rows(0, c)

    def gathered_z(l):
        got(g.at[l, c, :, 0, pl.ds(0, NZ - 1)], hz_r.at[l])
        block = g.at[l, c, :, y]
        for d in (1, 3, 2):
            send(block, block, hy_s, hy_r.at[l, d - 1], y_peer(d))
        send(block, block, hc_s, hc_r.at[l], core_peer)

    def gathered_own(l):
        for d in (1, 3, 2):
            block = g.at[l, c, :, (y + NY - d) % NY]
            got(block, hy_r.at[l, d - 1])
            send(block, block, hc_s, hc_r.at[l], core_peer)

    def gathered_other(l):
        got(g.at[l, oc], hc_r.at[l])

    def logits_part(l, cc, k):
        f[...] = g[l, cc].reshape(CHUNK * SUB, LANES).astype(F32)
        for j in range(SUB):
            h[rows_of(l, cc), j * LANES : (j + 1) * LANES] = f[pl.ds(j, CHUNK, stride=SUB), :].astype(BF16)
        out = jnp.dot(h[rows_of(l, cc), :], w[...], preferred_element_type=F32)
        part[k] = out.reshape(NX, GROUP, WIDTH)
        far = part.at[k, (x + 2) % NX]
        send(far.at[:, pl.ds(0, HALF)], relay.at[k, 0], rl_s, rl_r.at[k, 0], x_peer(1))
        send(far.at[:, pl.ds(HALF, HALF)], relay.at[k, 1], rl_s, rl_r.at[k, 1], x_peer(3))

    def logits_relay(k):
        right, left = (x + 1) % NX, (x + 3) % NX
        got(relay.at[k, 0], rl_r.at[k, 0])
        part[k, right, :, :HALF] = part[k, right, :, :HALF] + relay[k, 0]
        send(part.at[k, right], final.at[k, 0], fn_s, fn_r.at[k, 0], x_peer(1))
        got(relay.at[k, 1], rl_r.at[k, 1])
        part[k, left, :, HALF:] = part[k, left, :, HALF:] + relay[k, 1]
        send(part.at[k, left], final.at[k, 1], fn_s, fn_r.at[k, 1], x_peer(3))

    def softmax_part(l, cc, k):
        got(final.at[k, 0], fn_r.at[k, 0])
        got(final.at[k, 1], fn_r.at[k, 1])
        logits = part[k, x] + final[k, 0] + final[k, 1]
        peak = jnp.max(logits, axis=1, keepdims=True)
        raised = jnp.exp(logits - peak)
        total = jnp.sum(raised, axis=1, keepdims=True)
        here = columns == target_column(x, l, cc)
        hit = jnp.sum(jnp.where(here, logits, 0.0), axis=1, keepdims=True)
        u[l, cc, x] = jnp.where(here, 0.0, raised).astype(BF16)
        for i, value in enumerate((peak, total, hit)):
            line = jnp.sum(jnp.where(spot(l, cc), value, 0.0), axis=0, keepdims=True)
            st_send[l, 0, i : i + 1, :] = st_send[l, 0, i : i + 1, :] + line

    def raised_out(l, cc, k):
        for d in (1, 3, 2):
            send(u.at[l, cc, x], u.at[l, cc, x], ux_s, ux_r.at[k], x_peer(d))

    def merged(parts):
        peak = functools.reduce(jnp.maximum, [p[0:1] for p in parts])
        total = functools.reduce(jnp.add, [p[1:2] * jnp.exp(p[0:1] - peak) for p in parts])
        hit = functools.reduce(jnp.add, [p[2:3] for p in parts])
        return peak, total, hit

    def put(ref, values):
        for i, value in enumerate(values):
            ref[i : i + 1, :] = value

    def stats_core(l):
        send(st_send.at[l, 0], st_core.at[l], sc_s, sc_r.at[l], core_peer)

    def stats_y(l):
        got(st_core.at[l], sc_r.at[l])
        put(st_send.at[l, 1], merged([st_send[l, 0], st_core[l]]))
        st_y[l, y] = st_send[l, 1]
        for d in range(1, NY):
            send(st_send.at[l, 1], st_y.at[l, y], sy_s, sy_r.at[l], y_peer(d))

    def stats_z(l):
        got(st_y.at[l, pl.ds(0, NY - 1)], sy_r.at[l])
        put(st_send.at[l, 2], merged([st_y[l, i] for i in range(NY)]))
        st_z[l, z] = st_send[l, 2]
        for d in range(1, NZ):
            send(st_send.at[l, 2], st_z.at[l, z], sz_s, sz_r.at[l], z_peer(d))

    weight = 4.0 * (jnp.full((1, LANES), scale[0], jnp.int32).astype(F32) + 1.0)

    def stats_x(l):
        got(st_z.at[l, pl.ds(0, NZ - 1)], sz_r.at[l])
        peak, total, hit = merged([st_z[l, i] for i in range(NZ)])
        mine = lax.broadcasted_iota(jnp.int32, (1, LANES), 1) // 64 == l
        lse = peak + jnp.log(jnp.where(mine, total, 1.0))
        st_x[l, x, 0:1, :] = weight * jnp.exp(st_send[l, 0, 0:1, :] - lse)
        st_x[l, x, 1:2, :] = weight * (jnp.exp(hit - lse) - 1.0)
        for d in range(1, NX):
            send(st_x.at[l, x], st_x.at[l, x], sx_s, sx_r.at[l], x_peer(d))
        return jnp.sum(jnp.where(mine, lse - hit, 0.0), axis=1, keepdims=True)

    def product(l, cc, k):
        got(u.at[l, cc, pl.ds(0, 3)], ux_r.at[k])
        value = u[l, cc].reshape(CHUNK, WIDTH)
        raw[l, cc] = jnp.dot(value, wt[...], preferred_element_type=F32).reshape(NX, GROUP, FEAT)

    def scaled(l, cc, s):
        factor = as_column(st_x[l, s, 0:1, :], l, cc)
        entry = as_column(st_x[l, s, 1:2, :], l, cc)
        rows = pl.ds(s * GROUP, GROUP)
        return factor * raw[l, cc, s] + entry * hot_w[l, cc, rows, :].astype(F32)

    def hidden_core(l):
        got(st_x.at[l, pl.ds(0, NX - 1)], sx_r.at[l])
        for s in range(NX):
            core_out[l, s * GROUP : (s + 1) * GROUP, :] = scaled(l, oc, s).astype(BF16)
        send(core_out.at[l], core_in.at[l], gc_s, gc_r.at[l], core_peer)
        for s in range(NX):
            keep[l, s * GROUP : (s + 1) * GROUP, :] = scaled(l, c, s)

    def slab(l, py):
        for s in range(NX):
            rows = pl.ds(pl.multiple_of(s * GROUP + py * NZ, NZ), NZ)
            zf[pl.ds(s * NZ, NZ), :] = keep[l, rows, :]
        return zf[...]

    def hidden_y(l):
        got(core_in.at[l], gc_r.at[l])
        keep[l] = keep[l] + core_in[l].astype(F32)
        for d in (1, 3, 2):
            y_out[l, d - 1] = slab(l, (y + d) % NY).astype(BF16)
            send(y_out.at[l, d - 1], y_in.at[l, d - 1], gy_s, gy_r.at[l], y_peer(d))

    def hidden_z(l):
        got(y_in.at[l], gy_r.at[l])
        acc = slab(l, y)
        for d in range(1, NY):
            acc = acc + y_in[l, d - 1].astype(F32)
        for j in range(SUB):
            f[pl.ds(j, NX * NZ, stride=SUB), :] = acc[:, j * LANES : (j + 1) * LANES]
        z_out[l] = f[: NX * NZ * SUB, :].reshape(NX, NZ, SUB, LANES).astype(BF16)
        z_in[l, z] = z_out[l, :, z]
        for d in range(1, NZ):
            send(z_out.at[l, :, (z + d) % NZ], z_in.at[l, z], gz_s, gz_r.at[l], z_peer(d))

    def hidden_x(l):
        got(z_in.at[l, pl.ds(0, NZ - 1)], gz_r.at[l])
        acc = z_in[l, 0].astype(F32)
        for i in range(1, NZ):
            acc = acc + z_in[l, i].astype(F32)
        x_out[:, l] = acc.astype(BF16)

    def gradient(l, cc):
        for s in range(NX):
            factor = as_column(st_x[l, s, 0:1, :], l, cc)
            entry = as_column(st_x[l, s, 1:2, :], l, cc)
            here = columns == target_column(s, l, cc)
            value = jnp.where(here, entry, u[l, cc, s].astype(F32) * factor)
            at0 = pl.multiple_of((l * 2 + cc) * CHUNK + s * GROUP, GROUP)
            grad[pl.ds(at0, GROUP), :] = value.astype(BF16)

    gathered_z(0)
    target_rows(0, oc)
    gathered_z(1)
    target_rows(1, c)
    gathered_own(0)
    logits_part(0, c, 0)
    gathered_other(0)
    logits_part(0, oc, 1)
    target_rows(1, oc)
    logits_relay(0)
    logits_relay(1)
    gathered_own(1)
    logits_part(1, c, 2)
    gathered_other(1)
    logits_part(1, oc, 3)
    softmax_part(0, c, 0)
    softmax_part(0, oc, 1)
    stats_core(0)
    logits_relay(2)
    stats_y(0)
    logits_relay(3)
    raised_out(0, c, 0)
    raised_out(0, oc, 1)
    stats_z(0)
    softmax_part(1, c, 2)
    loss0 = stats_x(0)
    softmax_part(1, oc, 3)
    stats_core(1)
    raised_out(1, c, 2)
    raised_out(1, oc, 3)
    product(0, oc, 1)
    stats_y(1)
    product(0, c, 0)
    hidden_core(0)
    stats_z(1)
    hidden_y(0)
    product(1, oc, 3)
    product(1, c, 2)
    loss1 = stats_x(1)
    loss[...] = (loss0 + loss1) * (1.0 / 128.0)
    gradient(0, 0)
    gradient(0, 1)
    hidden_z(0)
    hidden_core(1)
    hidden_y(1)
    gradient(1, 0)
    gradient(1, 1)

    def head_tile(n, _):
        rows = pl.ds(pl.multiple_of(n * 512, 512), 512)
        out = lax.dot_general(
            h[:, rows], grad[...], (((0,), (0,)), ((), ())), preferred_element_type=F32
        )
        head[rows, :] = out.astype(BF16)
        return 0

    lax.fori_loop(0, FEAT // 512, head_tile, 0)
    hidden_x(0)
    hidden_z(1)
    hidden_x(1)
    x_in[x] = x_out[x]
    for d in range(1, NX):
        send(x_out.at[(x + d) % NX], x_in.at[x], gx_s, gx_r, x_peer(d))
    got(x_in.at[pl.ds(0, NX - 1)], gx_r)
    hs32[...] = x_in[...].astype(F32)
    for xx in range(NX):
        for k in range(SUB):
            at0 = xx * FEAT + k * LANES
            ghid[0, :, at0 : at0 + LANES] = hs32[xx, :, k, :].astype(BF16)

    got(hs.at[pl.ds(0, 3)], hx_s)
    got(tx.at[pl.ds(0, 3)], tx_s)
    got(g.at[:, 0, :, 0, pl.ds(0, NZ - 1)], hz_s)
    got(g.at[:, 0, :, pl.ds(0, NY - 1)], hy_s)
    got(g.at[:, 0], hc_s)
    got(relay, rl_s)
    got(final, fn_s)
    got(u.at[:, :, pl.ds(0, 3)], ux_s)
    got(st_core, sc_s)
    got(st_y.at[:, pl.ds(0, NY - 1)], sy_s)
    got(st_z.at[:, pl.ds(0, NZ - 1)], sz_s)
    got(st_x.at[:, pl.ds(0, NX - 1)], sx_s)
    got(core_in, gc_s)
    got(y_in, gy_s)
    got(z_in.at[:, pl.ds(0, NZ - 1)], gz_s)
    got(x_in.at[pl.ds(0, NX - 1)], gx_s)


def on_device(hidden, out_head, targets, scale_index):
    vmem = pltpu.VMEM
    dma = pltpu.SemaphoreType.DMA
    scratch = [
        vmem((FEAT, WIDTH), BF16),
        vmem((WIDTH, FEAT), BF16),
        vmem((NX, 2, SUB, LANES), F32),
        vmem((NX, 2, SUB, LANES), BF16),
        vmem((2, 2, NX, NY, NZ, SUB, LANES), BF16),
        vmem((CHUNK * SUB, LANES), F32),
        vmem((4 * CHUNK, FEAT), BF16),
        vmem((4, NX, GROUP, WIDTH), F32),
        vmem((4, 2, GROUP, HALF), F32),
        vmem((4, 2, GROUP, WIDTH), F32),
        vmem((2, 2, NX, GROUP, WIDTH), BF16),
        vmem((4 * CHUNK, WIDTH), BF16),
        vmem((CHUNK, WIDTH), BF16),
        vmem((2, 2, CHUNK, FEAT), BF16),
        vmem((2, 2, NX, GROUP, FEAT), F32),
        vmem((NX, 8, LANES), F32),
        vmem((2, 3, 8, LANES), F32),
        vmem((2, 8, LANES), F32),
        vmem((2, NY, 8, LANES), F32),
        vmem((2, NZ, 8, LANES), F32),
        vmem((2, NX, 8, LANES), F32),
        vmem((2, CHUNK, FEAT), BF16),
        vmem((2, CHUNK, FEAT), BF16),
        vmem((2, CHUNK, FEAT), F32),
        vmem((2, NY - 1, NX * NZ, FEAT), BF16),
        vmem((2, NY - 1, NX * NZ, FEAT), BF16),
        vmem((NX * NZ, FEAT), F32),
        vmem((2, NX, NZ, SUB, LANES), BF16),
        vmem((2, NZ, NX, SUB, LANES), BF16),
        vmem((NX, 2, SUB, LANES), BF16),
        vmem((NX, 2, SUB, LANES), BF16),
        dma, dma, dma, dma((2,)), dma((2, 3)), dma((2,)), dma((4, 2)), dma((4, 2)), dma((4,)),
        dma((2,)), dma((2,)), dma((2,)), dma((2,)), dma((2,)), dma((2,)), dma((2,)), dma,
    ] + [dma] * 16
    in_vmem = pl.BlockSpec(memory_space=pltpu.VMEM)
    head, ghid, loss = pl.pallas_call(
        kernel,
        out_shape=(
            jax.ShapeDtypeStruct((FEAT, WIDTH), BF16),
            jax.ShapeDtypeStruct(hidden.shape, BF16),
            jax.ShapeDtypeStruct((1, 1), F32),
        ),
        in_specs=[
            in_vmem,
            pl.BlockSpec(memory_space=pl.ANY),
            in_vmem,
            pl.BlockSpec(memory_space=pltpu.SMEM),
        ],
        out_specs=(in_vmem, in_vmem, in_vmem),
        scratch_shapes=scratch,
        compiler_params=pltpu.CompilerParams(
            collective_id=0, has_side_effects=True, vmem_limit_bytes=VMEM_MIB * 2**20
        ),
    )(hidden, out_head, targets, scale_index)
    return head, ghid, loss.reshape(1)


def solution(mesh):
    in_specs = (
        P("section", "vocab", None),
        P("section", "vocab"),
        P("section", None),
        P("section"),
    )
    out_specs = (P("section", "vocab"), P("section", "vocab", None), P("section"))
    return jax.shard_map(
        on_device, mesh=mesh, in_specs=in_specs, out_specs=out_specs, check_vma=False
    )
```

```python
import functools

import jax
import jax.numpy as jnp
from jax import lax
from jax.experimental import pallas as pl
from jax.experimental.pallas import tpu as pltpu
from jax.sharding import PartitionSpec as P

MESH = pl.DeviceIdType.MESH
F32 = jnp.float32
BF16 = jnp.bfloat16

NX, NZ, NY = 4, 8, 4
LANES = 128
SUB = 16
FEAT = SUB * LANES
WIDTH = 1024
HALF = WIDTH // 2
GROUP = 2 * NZ
CHUNK = NX * GROUP
PART = NY * CHUNK
VMEM_MIB = 46
Z_ORDER = (4, 3, 5, 2, 6, 1, 7)


def kernel(
    hid_hbm, w_hbm, tgt_hbm, scale, head, ghid, loss,
    hid, tgt, w, wt, hs32, hs, g, f, h, part, relay, final, u, grad, hot, hot_w,
    tx, st_raw, st_own, st_core, st_y, st_z, st_end,
    core_out, core_in, both, y_out, y_in, z_out, z_in, x_out, x_in,
    tcore_in, ty_out, ty_in, tz_out, tz_in,
    hid_sem, tgt_sem, w_sem, hx_r, tx_r, hz_r, hy_r, hc_r, rl_r, fn_r, ux_r,
    sc_r, sy_r, sz_r, sx_r, gc_r, gy_r, gz_r, gx_r,
    hx_s, tx_s, hz_s, hy_s, hc_s, rl_s, fn_s, ux_s,
    sc_s, sy_s, sz_s, sx_s, gc_s, gy_s, gz_s, gx_s, tc_r, ty_r, tz_r, tc_s, ty_s, tz_s,
):
    x = lax.axis_index("section")
    v = lax.axis_index("vocab")
    z, y, c = v // 8, (v // 2) % 4, v % 2
    oc = 1 - c

    def at(px, pz, py, pc):
        return (px, (pz * NY + py) * 2 + pc)

    def x_peer(d):
        return at((x + d) % NX, z, y, c)

    def y_peer(d):
        return at(x, z, (y + d) % NY, c)

    def z_peer(d):
        return at(x, (z + d) % NZ, y, c)

    core_peer = at(x, z, y, oc)

    def send(src, dst, s_sem, r_sem, peer):
        pltpu.make_async_remote_copy(
            src_ref=src, dst_ref=dst, send_sem=s_sem, recv_sem=r_sem,
            device_id=peer, device_id_type=MESH,
        ).start()

    def got(ref, sem):
        pltpu.make_async_copy(ref, ref, sem).wait()

    hid_copy = pltpu.make_async_copy(hid_hbm, hid, hid_sem)
    hid_copy.start()
    tgt_copy = pltpu.make_async_copy(tgt_hbm, tgt, tgt_sem)
    tgt_copy.start()
    barrier = pltpu.get_barrier_semaphore()
    peers = (
        [x_peer(d) for d in range(1, NX)]
        + [core_peer]
        + [y_peer(d) for d in range(1, NY)]
        + [z_peer(d) for d in range(1, NZ)]
    )
    for peer in peers:
        pl.semaphore_signal(barrier, inc=1, device_id=peer, device_id_type=MESH)

    w_copy = pltpu.make_async_copy(w_hbm, w, w_sem)
    w_copy.start()

    hid_copy.wait()
    own = hid[0].astype(F32)
    for xx in range(NX):
        for k in range(SUB):
            at0 = xx * FEAT + k * LANES
            hs32[xx, :, k, :] = own[:, at0 : at0 + LANES]
    hs[...] = hs32[...].astype(BF16)

    tgt_copy.wait()
    place = lax.broadcasted_iota(jnp.int32, (128, 128), 0)
    row = lax.broadcasted_iota(jnp.int32, (128, 128), 1)
    pl_l, pl_y, pl_c, pl_z = place // 64, (place // 16) % 4, (place // 8) % 2, place % 8
    match = row == pl_z * 16 + pl_y * 4 + pl_c * 2 + pl_l
    tcol_all = jnp.sum(
        jnp.where(match, tgt[...].astype(F32), 0.0), axis=1, keepdims=True
    )
    weight = 4.0 * (jnp.full((1, LANES), scale[0], jnp.int32).astype(F32) + 1.0)
    tx[x] = jnp.zeros((8, LANES), F32)
    tx[x, 0:1, :] = jnp.sum(jnp.where(place == row, tcol_all, 0.0), axis=0, keepdims=True)
    tx[x, 1:2, :] = weight
    st_raw[...] = jnp.zeros_like(st_raw)
    st_own[...] = jnp.zeros_like(st_own)

    pl.semaphore_wait(barrier, len(peers))

    for d in range(1, NX):
        send(hs.at[(x + d) % NX], g.at[:, y, x, c, z], hx_s, hx_r, x_peer(d))
    for d in range(1, NX):
        send(tx.at[x], tx.at[x], tx_s, tx_r, x_peer(d))
    for l in range(2):
        g[l, y, x, c, z] = hs[x, l]
    got(hs.at[pl.ds(0, 3)], hx_r)

    for l in range(2):
        for d in Z_ORDER:
            piece = g.at[l, y, :, c, z]
            send(piece, piece, hz_s, hz_r.at[l], z_peer(d))

    columns = v * WIDTH + lax.broadcasted_iota(jnp.int32, (GROUP, WIDTH), 1)
    lane = lax.broadcasted_iota(jnp.int32, (GROUP, LANES), 1)
    sub = lax.broadcasted_iota(jnp.int32, (GROUP, LANES), 0)

    def spot(s, py):
        return lane == sub + (s % 2) * 64 + py * GROUP

    def as_column(lines, s, py):
        line = lines[s // 2 : s // 2 + 1]
        return jnp.sum(jnp.where(spot(s, py), line, 0.0), axis=1, keepdims=True)

    def target_column(s, l, py):
        here = lane == sub + (l * NY + py) * GROUP
        return jnp.sum(jnp.where(here, tx[s, 0:1, :], 0.0), axis=1, keepdims=True).astype(jnp.int32)

    def rows_of(l, py, s=0, count=CHUNK):
        return pl.ds(pl.multiple_of((l * NY + py) * CHUNK + s * GROUP, GROUP), count)

    got(tx.at[pl.ds(0, 3)], tx_r)
    w_copy.wait()

    def turn(n, _):
        rows = pl.ds(pl.multiple_of(n * 512, 512), 512)
        wt[:, rows] = w[rows, :].T
        return 0

    lax.fori_loop(0, FEAT // 512, turn, 0)

    for l in range(2):
        for py in range(NY):
            for s in range(NX):
                here = columns == target_column(s, l, py)
                at0 = py * CHUNK + s * GROUP
                hot[at0 : at0 + GROUP, :] = jnp.where(here, 1.0, 0.0).astype(BF16)
        out = jnp.dot(hot[...], wt[...], preferred_element_type=F32)
        for cc in range(2):
            for py in range(NY):
                for s in range(0, NX, 2):
                    at0 = [py * CHUNK + (s + i) * GROUP + cc * NZ for i in range(2)]
                    pair = jnp.concatenate([out[i : i + NZ] for i in at0], axis=0)
                    hot_w[l, cc, py, s * NZ : (s + 2) * NZ, :] = pair.astype(BF16)

    def from_y(d):
        return (y + NY - d) % NY

    def gathered_z(l):
        got(g.at[l, 0, :, 0, pl.ds(0, NZ - 1)], hz_r.at[l])
        block = g.at[l, y, :, c]
        for d in (1, 3, 2):
            send(block, block, hy_s, hy_r.at[l, d - 1], y_peer(d))
        send(block, block, hc_s, hc_r.at[l, 0], core_peer)

    def gathered_y(l, d):
        block = g.at[l, from_y(d), :, c]
        got(block, hy_r.at[l, d - 1])
        send(block, block, hc_s, hc_r.at[l, d], core_peer)

    def logits_part(l, d):
        py, k = from_y(d), l * NY + d
        got(g.at[l, py, :, oc], hc_r.at[l, d])
        f[...] = g[l, py].reshape(CHUNK * SUB, LANES).astype(F32)
        rows = rows_of(l, py)
        for j in range(SUB):
            h[rows, j * LANES : (j + 1) * LANES] = f[pl.ds(j, CHUNK, stride=SUB), :].astype(BF16)
        out = jnp.dot(h[rows, :], w[...], preferred_element_type=F32)
        part[k] = out.reshape(NX, GROUP, WIDTH)
        far = part.at[k, (x + 2) % NX]
        send(far.at[:, pl.ds(0, HALF)], relay.at[k, 0], rl_s, rl_r.at[k, 0], x_peer(1))
        send(far.at[:, pl.ds(HALF, HALF)], relay.at[k, 1], rl_s, rl_r.at[k, 1], x_peer(3))

    def logits_relay(l, d):
        k = l * NY + d
        right, left = (x + 1) % NX, (x + 3) % NX
        got(relay.at[k, 0], rl_r.at[k, 0])
        part[k, right, :, :HALF] = part[k, right, :, :HALF] + relay[k, 0]
        send(part.at[k, right], final.at[k, 0], fn_s, fn_r.at[k, 0], x_peer(1))
        got(relay.at[k, 1], rl_r.at[k, 1])
        part[k, left, :, HALF:] = part[k, left, :, HALF:] + relay[k, 1]
        send(part.at[k, left], final.at[k, 1], fn_s, fn_r.at[k, 1], x_peer(3))

    def softmax_part(l, d):
        py, k = from_y(d), l * NY + d
        got(final.at[k, 0], fn_r.at[k, 0])
        got(final.at[k, 1], fn_r.at[k, 1])
        logits = part[k, x] + final[k, 0] + final[k, 1]
        peak = jnp.max(logits, axis=1, keepdims=True)
        raised = jnp.exp(logits - peak)
        total = jnp.sum(raised, axis=1, keepdims=True)
        here = columns == target_column(x, l, py)
        hit = jnp.sum(jnp.where(here, logits, 0.0), axis=1, keepdims=True)
        u[l, py, x] = jnp.where(here, 0.0, raised).astype(BF16)
        tile = st_raw[l, x]
        which = lax.broadcasted_iota(jnp.int32, (8, LANES), 0)
        for i, value in enumerate((peak, total, hit)):
            line = jnp.sum(jnp.where(spot(x, py), value, 0.0), axis=0, keepdims=True)
            tile = tile + jnp.where(which == 2 * i + x // 2, line, 0.0)
        st_raw[l, x] = tile

    def raised_out(l, d):
        mine = u.at[l, from_y(d), x]
        for other in (1, 3, 2):
            send(mine, mine, ux_s, ux_r.at[l, d], x_peer(other))

    def merged(parts):
        peak = functools.reduce(jnp.maximum, [p[0:2] for p in parts])
        total = functools.reduce(jnp.add, [p[2:4] * jnp.exp(p[0:2] - peak) for p in parts])
        hit = functools.reduce(jnp.add, [p[4:6] for p in parts])
        return peak, total, hit

    def put(ref, values):
        for i, value in enumerate(values):
            ref[2 * i : 2 * i + 2, :] = value

    def stats_x(l):
        for d in range(1, NX):
            send(st_raw.at[l, x], st_raw.at[l, x], sx_s, sx_r.at[l], x_peer(d))

    def stats_core(l):
        got(st_raw.at[l, pl.ds(0, NX - 1)], sx_r.at[l])
        st_own[l, 0] = st_raw[l, 0] + st_raw[l, 1] + st_raw[l, 2] + st_raw[l, 3]
        send(st_own.at[l, 0], st_core.at[l], sc_s, sc_r.at[l], core_peer)

    def stats_y(l):
        got(st_core.at[l], sc_r.at[l])
        put(st_own.at[l, 1], merged([st_own[l, 0], st_core[l]]))
        st_y[l, y] = st_own[l, 1]
        for d in range(1, NY):
            send(st_own.at[l, 1], st_y.at[l, y], sy_s, sy_r.at[l], y_peer(d))

    def stats_z(l):
        got(st_y.at[l, pl.ds(0, NY - 1)], sy_r.at[l])
        put(st_own.at[l, 2], merged([st_y[l, i] for i in range(NY)]))
        st_z[l, z] = st_own[l, 2]
        for d in Z_ORDER:
            send(st_own.at[l, 2], st_z.at[l, z], sz_s, sz_r.at[l], z_peer(d))

    def stats_end(l):
        got(st_z.at[l, pl.ds(0, NZ - 1)], sz_r.at[l])
        peak, total, hit = merged([st_z[l, i] for i in range(NZ)])
        lse = peak + jnp.log(total)
        lower = lax.broadcasted_iota(jnp.int32, (1, LANES), 1) < 64
        lines = [jnp.where(lower, tx[s, 1:2, :], tx[s + 1, 1:2, :]) for s in (0, 2)]
        weights = jnp.concatenate(lines, axis=0)
        st_end[l, 0:2, :] = weights * jnp.exp(st_own[l, 0, 0:2, :] - lse)
        st_end[l, 2:4, :] = weights * (jnp.exp(hit - lse) - 1.0)
        st_end[l, 4:6, :] = lse
        st_end[l, 6:8, :] = weights
        mine = (lax.broadcasted_iota(jnp.int32, (2, LANES), 1) // 64 == x % 2) & (
            lax.broadcasted_iota(jnp.int32, (2, LANES), 0) == x // 2
        )
        gap = jnp.where(mine, lse - hit, 0.0)
        return jnp.sum(gap[0:1] + gap[1:2], axis=1, keepdims=True)

    small = lax.broadcasted_iota(jnp.int32, (NZ, LANES), 1)
    small_sub = lax.broadcasted_iota(jnp.int32, (NZ, LANES), 0)

    def own_column(lines, py):
        parts = []
        for s in range(NX):
            here = small == small_sub + (s % 2) * 64 + py * GROUP + c * NZ
            line = lines[s // 2 : s // 2 + 1]
            parts.append(jnp.sum(jnp.where(here, line, 0.0), axis=1, keepdims=True))
        return jnp.concatenate(parts, axis=0)

    def product(l, d):
        py = from_y(d)
        got(u.at[l, py, pl.ds(0, NX - 1)], ux_r.at[l, d])
        out = jnp.dot(u[l, py].reshape(CHUNK, WIDTH), wt[...], preferred_element_type=F32)
        for s in range(NX):
            for cc in range(2):
                at0 = s * GROUP + cc * NZ
                both[l, cc, py, s * NZ : (s + 1) * NZ, :] = out[at0 : at0 + NZ]
        core_out[l, py] = both[l, oc, py].astype(BF16)
        send(core_out.at[l, py], core_in.at[l, py], gc_s, gc_r.at[l, d], core_peer)

    def chip_sum(l, py):
        peak = st_own[l, 1, 0:2, :]
        mine = own_column(jnp.exp(st_own[l, 0, 0:2, :] - peak), py)
        other = own_column(jnp.exp(st_core[l, 0:2, :] - peak), py)
        return mine * both[l, c, py] + other * core_in[l, py].astype(F32)

    def hidden_y(l, d):
        py = from_y(d)
        got(core_in.at[l, py], gc_r.at[l, d])
        y_out[l, d - 1] = chip_sum(l, py).astype(BF16)
        send(y_out.at[l, d - 1], y_in.at[l, d - 1], gy_s, gy_r.at[l], y_peer(NY - d))

    def as_tiles(acc, out):
        for j in range(SUB):
            f[pl.ds(j, NX * NZ, stride=SUB), :] = acc[:, j * LANES : (j + 1) * LANES]
        out[...] = f[: NX * NZ * SUB, :].reshape(NX, NZ, SUB, LANES).astype(BF16)

    def hidden_z(l):
        got(core_in.at[l, y], gc_r.at[l, 0])
        got(y_in.at[l], gy_r.at[l])
        lse, weights = st_end[l, 4:6, :], st_end[l, 6:8, :]
        acc = own_column(weights * jnp.exp(st_y[l, y, 0:2, :] - lse), y) * chip_sum(l, y)
        for d in range(1, NY):
            factor = own_column(weights * jnp.exp(st_y[l, (y + d) % NY, 0:2, :] - lse), y)
            acc = acc + factor * y_in[l, d - 1].astype(F32)
        as_tiles(acc, z_out.at[l])
        z_in[l, z] = z_out[l, :, z]
        for d in Z_ORDER:
            send(z_out.at[l, :, (z + d) % NZ], z_in.at[l, z], gz_s, gz_r.at[l], z_peer(d))

    def hidden_x(l):
        got(z_in.at[l, pl.ds(0, NZ - 1)], gz_r.at[l])
        acc = z_in[l, 0].astype(F32)
        for i in range(1, NZ):
            acc = acc + z_in[l, i].astype(F32)
        at_target = tz_in[l, 0].astype(F32)
        for i in range(1, NZ):
            at_target = at_target + tz_in[l, i].astype(F32)
        line_at = lax.broadcasted_iota(jnp.int32, (1, LANES), 1)
        for s in range(NX):
            here = line_at == (s % 2) * 64 + y * GROUP + c * NZ + z
            line = st_end[l, 2 + s // 2 : 3 + s // 2, :]
            entry = jnp.sum(jnp.where(here, line, 0.0), axis=1, keepdims=True)
            x_out[s, l] = (acc[s] + entry * at_target[s]).astype(BF16)

    def target_core(l):
        send(hot_w.at[l, oc], tcore_in.at[l], tc_s, tc_r.at[l], core_peer)

    def target_y(l):
        got(tcore_in.at[l], tc_r.at[l])
        for d in (1, 3, 2):
            py = (y + d) % NY
            ty_out[l, d - 1] = (hot_w[l, c, py].astype(F32) + tcore_in[l, py].astype(F32)).astype(BF16)
            send(ty_out.at[l, d - 1], ty_in.at[l, d - 1], ty_s, ty_r.at[l], y_peer(d))

    def target_z(l):
        got(ty_in.at[l], ty_r.at[l])
        acc = hot_w[l, c, y].astype(F32) + tcore_in[l, y].astype(F32)
        for d in range(1, NY):
            acc = acc + ty_in[l, d - 1].astype(F32)
        as_tiles(acc, tz_out.at[l])
        tz_in[l, z] = tz_out[l, :, z]
        for d in Z_ORDER:
            send(tz_out.at[l, :, (z + d) % NZ], tz_in.at[l, z], tz_s, tz_r.at[l], z_peer(d))

    def target_end(l):
        got(tz_in.at[l, pl.ds(0, NZ - 1)], tz_r.at[l])

    def gradient(l):
        for py in range(NY):
            for s in range(NX):
                factor = as_column(st_end[l, 0:2, :], s, py)
                entry = as_column(st_end[l, 2:4, :], s, py)
                here = columns == target_column(s, l, py)
                value = jnp.where(here, entry, u[l, py, s].astype(F32) * factor)
                grad[rows_of(l, py, s, GROUP), :] = value.astype(BF16)

    gathered_z(0)
    logits_part(0, 0)
    gathered_z(1)
    logits_part(1, 0)
    target_core(0)
    gathered_y(0, 1)
    gathered_y(0, 3)
    logits_relay(0, 0)
    logits_part(0, 1)
    logits_relay(1, 0)
    logits_part(0, 3)
    gathered_y(0, 2)
    target_core(1)
    logits_part(0, 2)
    target_y(0)
    softmax_part(0, 0)
    raised_out(0, 0)
    gathered_y(1, 1)
    logits_relay(0, 1)
    gathered_y(1, 3)
    logits_part(1, 1)
    logits_relay(0, 3)
    softmax_part(1, 0)
    logits_part(1, 3)
    logits_relay(0, 2)
    gathered_y(1, 2)
    target_y(1)
    softmax_part(0, 1)
    raised_out(0, 1)
    logits_part(1, 2)
    softmax_part(0, 3)
    raised_out(0, 3)
    logits_relay(1, 1)
    logits_relay(1, 3)
    product(0, 0)
    softmax_part(0, 2)
    stats_x(0)
    logits_relay(1, 2)
    raised_out(0, 2)
    product(0, 1)
    product(0, 3)
    softmax_part(1, 1)
    raised_out(1, 1)
    softmax_part(1, 3)
    raised_out(1, 3)
    stats_core(0)
    softmax_part(1, 2)
    stats_x(1)
    raised_out(1, 2)
    raised_out(1, 0)
    stats_y(0)
    target_z(0)
    hidden_y(0, 1)
    hidden_y(0, 3)
    product(0, 2)
    hidden_y(0, 2)
    stats_z(0)
    target_z(1)
    product(1, 1)
    stats_core(1)
    product(1, 3)
    stats_y(1)
    hidden_y(1, 1)
    hidden_y(1, 3)
    product(1, 2)
    hidden_y(1, 2)
    loss0 = stats_end(0)
    product(1, 0)
    stats_z(1)
    hidden_z(0)
    loss1 = stats_end(1)
    hidden_z(1)
    gradient(0)
    gradient(1)
    loss[...] = (loss0 + loss1) * (1.0 / 128.0)

    def head_tile(n, _):
        rows = pl.ds(pl.multiple_of(n * 512, 512), 512)
        out = lax.dot_general(
            h[:, rows], grad[...], (((0,), (0,)), ((), ())), preferred_element_type=F32
        )
        head[rows, :] = out.astype(BF16)
        return 0

    lax.fori_loop(0, FEAT // 512, head_tile, 0)
    target_end(0)
    target_end(1)
    hidden_x(0)
    hidden_x(1)
    x_in[x] = x_out[x]
    for d in range(1, NX):
        send(x_out.at[(x + d) % NX], x_in.at[x], gx_s, gx_r, x_peer(d))
    got(x_in.at[pl.ds(0, NX - 1)], gx_r)
    hs32[...] = x_in[...].astype(F32)
    for xx in range(NX):
        for k in range(SUB):
            at0 = xx * FEAT + k * LANES
            ghid[0, :, at0 : at0 + LANES] = hs32[xx, :, k, :].astype(BF16)

    got(hs.at[pl.ds(0, 3)], hx_s)
    got(tx.at[pl.ds(0, 3)], tx_s)
    got(g.at[:, 0, :, 0, pl.ds(0, NZ - 1)], hz_s)
    got(g.at[:, pl.ds(0, NY - 1), :, 0], hy_s)
    got(g.at[:, :, :, 0], hc_s)
    got(relay, rl_s)
    got(final, fn_s)
    got(u.at[:, :, pl.ds(0, NX - 1)], ux_s)
    got(st_core, sc_s)
    got(st_y.at[:, pl.ds(0, NY - 1)], sy_s)
    got(st_z.at[:, pl.ds(0, NZ - 1)], sz_s)
    got(st_raw.at[:, pl.ds(0, NX - 1)], sx_s)
    got(tcore_in, tc_s)
    got(ty_in, ty_s)
    got(tz_in.at[:, pl.ds(0, NZ - 1)], tz_s)
    got(core_in, gc_s)
    got(y_in, gy_s)
    got(z_in.at[:, pl.ds(0, NZ - 1)], gz_s)
    got(x_in.at[pl.ds(0, NX - 1)], gx_s)


def on_device(hidden, out_head, targets, scale_index):
    vmem = pltpu.VMEM
    dma = pltpu.SemaphoreType.DMA
    scratch = [
        vmem((1, 2, NX * FEAT), BF16),
        vmem((1, LANES), jnp.int32),
        vmem((FEAT, WIDTH), BF16),
        vmem((WIDTH, FEAT), BF16),
        vmem((NX, 2, SUB, LANES), F32),
        vmem((NX, 2, SUB, LANES), BF16),
        vmem((2, NY, NX, 2, NZ, SUB, LANES), BF16),
        vmem((CHUNK * SUB, LANES), F32),
        vmem((2 * PART, FEAT), BF16),
        vmem((2 * NY, NX, GROUP, WIDTH), F32),
        vmem((2 * NY, 2, GROUP, HALF), F32),
        vmem((2 * NY, 2, GROUP, WIDTH), F32),
        vmem((2, NY, NX, GROUP, WIDTH), BF16),
        vmem((2 * PART, WIDTH), BF16),
        vmem((PART, WIDTH), BF16),
        vmem((2, 2, NY, NX * NZ, FEAT), BF16),
        vmem((NX, 8, LANES), F32),
        vmem((2, NX, 8, LANES), F32),
        vmem((2, 3, 8, LANES), F32),
        vmem((2, 8, LANES), F32),
        vmem((2, NY, 8, LANES), F32),
        vmem((2, NZ, 8, LANES), F32),
        vmem((2, 8, LANES), F32),
        vmem((2, NY, NX * NZ, FEAT), BF16),
        vmem((2, NY, NX * NZ, FEAT), BF16),
        vmem((2, 2, NY, NX * NZ, FEAT), F32),
        vmem((2, NY - 1, NX * NZ, FEAT), BF16),
        vmem((2, NY - 1, NX * NZ, FEAT), BF16),
        vmem((2, NX, NZ, SUB, LANES), BF16),
        vmem((2, NZ, NX, SUB, LANES), BF16),
        vmem((NX, 2, SUB, LANES), BF16),
        vmem((NX, 2, SUB, LANES), BF16),
        vmem((2, NY, NX * NZ, FEAT), BF16),
        vmem((2, NY - 1, NX * NZ, FEAT), BF16),
        vmem((2, NY - 1, NX * NZ, FEAT), BF16),
        vmem((2, NX, NZ, SUB, LANES), BF16),
        vmem((2, NZ, NX, SUB, LANES), BF16),
        dma, dma, dma, dma, dma, dma((2,)), dma((2, 3)), dma((2, 4)), dma((8, 2)), dma((8, 2)), dma((2, 4)),
        dma((2,)), dma((2,)), dma((2,)), dma((2,)), dma((2, 4)), dma((2,)), dma((2,)), dma,
    ] + [dma] * 16 + [dma((2,))] * 3 + [dma] * 3
    in_hbm = pl.BlockSpec(memory_space=pltpu.HBM)
    in_vmem = pl.BlockSpec(memory_space=pltpu.VMEM)
    head, ghid, loss = pl.pallas_call(
        kernel,
        out_shape=(
            jax.ShapeDtypeStruct((FEAT, WIDTH), BF16),
            jax.ShapeDtypeStruct(hidden.shape, BF16),
            jax.ShapeDtypeStruct((1, 1), F32),
        ),
        in_specs=[
            in_hbm,
            in_hbm,
            in_hbm,
            pl.BlockSpec(memory_space=pltpu.SMEM),
        ],
        out_specs=(in_vmem, in_vmem, in_vmem),
        scratch_shapes=scratch,
        compiler_params=pltpu.CompilerParams(
            collective_id=0, has_side_effects=True, vmem_limit_bytes=VMEM_MIB * 2**20
        ),
    )(hidden, out_head, targets, scale_index)
    return head, ghid, loss.reshape(1)


def solution(mesh):
    in_specs = (
        P("section", "vocab", None),
        P("section", "vocab"),
        P("section", None),
        P("section"),
    )
    out_specs = (P("section", "vocab"), P("section", "vocab", None), P("section"))
    return jax.shard_map(
        on_device, mesh=mesh, in_specs=in_specs, out_specs=out_specs, check_vma=False
    )
```

```python
import functools

import jax
import jax.numpy as jnp
from jax import lax
from jax.experimental import pallas as pl
from jax.experimental.pallas import tpu as pltpu
from jax.sharding import PartitionSpec as P

MESH = pl.DeviceIdType.MESH
F32 = jnp.float32
BF16 = jnp.bfloat16

NX, NZ, NY = 4, 8, 4
LANES = 128
SUB = 16
FEAT = SUB * LANES
WIDTH = 1024
HALF = WIDTH // 2
GROUP = 2 * NZ
CHUNK = NX * GROUP
PART = NY * CHUNK
VMEM_MIB = 46
Z_ORDER = (4, 3, 5, 2, 6, 1, 7)


def kernel(
    hid_hbm, w_hbm, tgt_hbm, scale, head, ghid, loss,
    hid, tgt, w, wt, hs32, hs, g, f, h, part, relay, final, u, grad, hot, hot_w,
    tx, st_raw, st_own, st_core, st_y, st_z, st_end,
    core_out, core_in, both, y_out, y_in, z_out, z_in, x_out, x_in,
    tcore_in, ty_out, ty_in, tz_out, tz_in,
    hid_sem, tgt_sem, w_sem, hx_r, tx_r, hz_r, hy_r, hc_r, rl_r, fn_r, ux_r,
    sc_r, sy_r, sz_r, sx_r, gc_r, gy_r, gz_r, gx_r,
    hx_s, tx_s, hz_s, hy_s, hc_s, rl_s, fn_s, ux_s,
    sc_s, sy_s, sz_s, sx_s, gc_s, gy_s, gz_s, gx_s, tc_r, ty_r, tz_r, tc_s, ty_s, tz_s,
):
    x = lax.axis_index("section")
    v = lax.axis_index("vocab")
    z, y, c = v // 8, (v // 2) % 4, v % 2
    oc = 1 - c

    def at(px, pz, py, pc):
        return (px, (pz * NY + py) * 2 + pc)

    def x_peer(d):
        return at((x + d) % NX, z, y, c)

    def y_peer(d):
        return at(x, z, (y + d) % NY, c)

    def z_peer(d):
        return at(x, (z + d) % NZ, y, c)

    core_peer = at(x, z, y, oc)

    def send(src, dst, s_sem, r_sem, peer):
        pltpu.make_async_remote_copy(
            src_ref=src, dst_ref=dst, send_sem=s_sem, recv_sem=r_sem,
            device_id=peer, device_id_type=MESH,
        ).start()

    def got(ref, sem):
        pltpu.make_async_copy(ref, ref, sem).wait()

    hid_copy = pltpu.make_async_copy(hid_hbm, hid, hid_sem)
    hid_copy.start()
    tgt_copy = pltpu.make_async_copy(tgt_hbm, tgt, tgt_sem)
    tgt_copy.start()
    barrier = pltpu.get_barrier_semaphore()
    peers = (
        [x_peer(d) for d in range(1, NX)]
        + [core_peer]
        + [y_peer(d) for d in range(1, NY)]
        + [z_peer(d) for d in range(1, NZ)]
    )
    for peer in peers:
        pl.semaphore_signal(barrier, inc=1, device_id=peer, device_id_type=MESH)

    w_copy = pltpu.make_async_copy(w_hbm, w, w_sem)
    w_copy.start()

    hid_copy.wait()
    own = hid[0].astype(F32)
    for xx in range(NX):
        for k in range(SUB):
            at0 = xx * FEAT + k * LANES
            hs32[xx, :, k, :] = own[:, at0 : at0 + LANES]
    hs[...] = hs32[...].astype(BF16)

    tgt_copy.wait()
    place = lax.broadcasted_iota(jnp.int32, (128, 128), 0)
    row = lax.broadcasted_iota(jnp.int32, (128, 128), 1)
    pl_l, pl_y, pl_c, pl_z = place // 64, (place // 16) % 4, (place // 8) % 2, place % 8
    match = row == pl_z * 16 + pl_y * 4 + pl_c * 2 + pl_l
    tcol_all = jnp.sum(
        jnp.where(match, tgt[...].astype(F32), 0.0), axis=1, keepdims=True
    )
    weight = 4.0 * (jnp.full((1, LANES), scale[0], jnp.int32).astype(F32) + 1.0)
    tx[x] = jnp.zeros((8, LANES), F32)
    tx[x, 0:1, :] = jnp.sum(jnp.where(place == row, tcol_all, 0.0), axis=0, keepdims=True)
    tx[x, 1:2, :] = weight
    st_raw[...] = jnp.zeros_like(st_raw)
    st_own[...] = jnp.zeros_like(st_own)

    pl.semaphore_wait(barrier, len(peers))

    for d in range(1, NX):
        send(hs.at[(x + d) % NX], g.at[:, y, x, c, z], hx_s, hx_r, x_peer(d))
    for d in range(1, NX):
        send(tx.at[x], tx.at[x], tx_s, tx_r, x_peer(d))
    for l in range(2):
        g[l, y, x, c, z] = hs[x, l]
    got(hs.at[pl.ds(0, 3)], hx_r)

    for l in range(2):
        for d in Z_ORDER:
            piece = g.at[l, y, :, c, z]
            send(piece, piece, hz_s, hz_r.at[l], z_peer(d))

    columns = v * WIDTH + lax.broadcasted_iota(jnp.int32, (GROUP, WIDTH), 1)
    lane = lax.broadcasted_iota(jnp.int32, (GROUP, LANES), 1)
    sub = lax.broadcasted_iota(jnp.int32, (GROUP, LANES), 0)

    def spot(s, py):
        return lane == sub + (s % 2) * 64 + py * GROUP

    def as_column(lines, s, py):
        line = lines[s // 2 : s // 2 + 1]
        return jnp.sum(jnp.where(spot(s, py), line, 0.0), axis=1, keepdims=True)

    def target_column(s, l, py):
        here = lane == sub + (l * NY + py) * GROUP
        return jnp.sum(jnp.where(here, tx[s, 0:1, :], 0.0), axis=1, keepdims=True).astype(jnp.int32)

    def rows_of(l, py, s=0, count=CHUNK):
        return pl.ds(pl.multiple_of((l * NY + py) * CHUNK + s * GROUP, GROUP), count)

    got(tx.at[pl.ds(0, 3)], tx_r)
    w_copy.wait()

    def turn(n, _):
        rows = pl.ds(pl.multiple_of(n * 512, 512), 512)
        wt[:, rows] = w[rows, :].T
        return 0

    lax.fori_loop(0, FEAT // 512, turn, 0)

    for l in range(2):
        for py in range(NY):
            for s in range(NX):
                here = columns == target_column(s, l, py)
                at0 = py * CHUNK + s * GROUP
                hot[at0 : at0 + GROUP, :] = jnp.where(here, 1.0, 0.0).astype(BF16)
        out = jnp.dot(hot[...], wt[...], preferred_element_type=F32)
        for cc in range(2):
            for py in range(NY):
                for s in range(0, NX, 2):
                    at0 = [py * CHUNK + (s + i) * GROUP + cc * NZ for i in range(2)]
                    pair = jnp.concatenate([out[i : i + NZ] for i in at0], axis=0)
                    hot_w[l, cc, py, s * NZ : (s + 2) * NZ, :] = pair.astype(BF16)

    def from_y(d):
        return (y + NY - d) % NY

    def gathered_z(l):
        got(g.at[l, 0, :, 0, pl.ds(0, NZ - 1)], hz_r.at[l])
        block = g.at[l, y, :, c]
        for d in (1, 3, 2):
            send(block, block, hy_s, hy_r.at[l, d - 1], y_peer(d))
        send(block, block, hc_s, hc_r.at[l, 0], core_peer)

    def gathered_y(l, d):
        block = g.at[l, from_y(d), :, c]
        got(block, hy_r.at[l, d - 1])
        send(block, block, hc_s, hc_r.at[l, d], core_peer)

    def logits_part(l, d):
        py, k = from_y(d), l * NY + d
        got(g.at[l, py, :, oc], hc_r.at[l, d])
        f[...] = g[l, py].reshape(CHUNK * SUB, LANES).astype(F32)
        rows = rows_of(l, py)
        for j in range(SUB):
            h[rows, j * LANES : (j + 1) * LANES] = f[pl.ds(j, CHUNK, stride=SUB), :].astype(BF16)
        out = jnp.dot(h[rows, :], w[...], preferred_element_type=F32)
        part[k] = out.reshape(NX, GROUP, WIDTH)
        far = part.at[k, (x + 2) % NX]
        send(far.at[:, pl.ds(0, HALF)], relay.at[k, 0], rl_s, rl_r.at[k, 0], x_peer(1))
        send(far.at[:, pl.ds(HALF, HALF)], relay.at[k, 1], rl_s, rl_r.at[k, 1], x_peer(3))

    def logits_relay(l, d):
        k = l * NY + d
        right, left = (x + 1) % NX, (x + 3) % NX
        got(relay.at[k, 0], rl_r.at[k, 0])
        part[k, right, :, :HALF] = part[k, right, :, :HALF] + relay[k, 0]
        send(part.at[k, right], final.at[k, 0], fn_s, fn_r.at[k, 0], x_peer(1))
        got(relay.at[k, 1], rl_r.at[k, 1])
        part[k, left, :, HALF:] = part[k, left, :, HALF:] + relay[k, 1]
        send(part.at[k, left], final.at[k, 1], fn_s, fn_r.at[k, 1], x_peer(3))

    def softmax_part(l, d):
        py, k = from_y(d), l * NY + d
        got(final.at[k, 0], fn_r.at[k, 0])
        got(final.at[k, 1], fn_r.at[k, 1])
        logits = part[k, x] + final[k, 0] + final[k, 1]
        peak = jnp.max(logits, axis=1, keepdims=True)
        raised = jnp.exp(logits - peak)
        total = jnp.sum(raised, axis=1, keepdims=True)
        here = columns == target_column(x, l, py)
        hit = jnp.sum(jnp.where(here, logits, 0.0), axis=1, keepdims=True)
        u[l, py, x] = jnp.where(here, 0.0, raised).astype(BF16)
        tile = st_raw[l, x]
        which = lax.broadcasted_iota(jnp.int32, (8, LANES), 0)
        for i, value in enumerate((peak, total, hit)):
            line = jnp.sum(jnp.where(spot(x, py), value, 0.0), axis=0, keepdims=True)
            tile = tile + jnp.where(which == 2 * i + x // 2, line, 0.0)
        st_raw[l, x] = tile

    def raised_out(l, d):
        mine = u.at[l, from_y(d), x]
        for other in (1, 3, 2):
            send(mine, mine, ux_s, ux_r.at[l, d], x_peer(other))

    def merged(parts):
        peak = functools.reduce(jnp.maximum, [p[0:2] for p in parts])
        total = functools.reduce(jnp.add, [p[2:4] * jnp.exp(p[0:2] - peak) for p in parts])
        hit = functools.reduce(jnp.add, [p[4:6] for p in parts])
        return peak, total, hit

    def put(ref, values):
        for i, value in enumerate(values):
            ref[2 * i : 2 * i + 2, :] = value

    def stats_x(l):
        for d in range(1, NX):
            send(st_raw.at[l, x], st_raw.at[l, x], sx_s, sx_r.at[l], x_peer(d))

    def stats_core(l):
        got(st_raw.at[l, pl.ds(0, NX - 1)], sx_r.at[l])
        st_own[l, 0] = st_raw[l, 0] + st_raw[l, 1] + st_raw[l, 2] + st_raw[l, 3]
        send(st_own.at[l, 0], st_core.at[l], sc_s, sc_r.at[l], core_peer)

    def stats_y(l):
        got(st_core.at[l], sc_r.at[l])
        put(st_own.at[l, 1], merged([st_own[l, 0], st_core[l]]))
        st_y[l, y] = st_own[l, 1]
        for d in range(1, NY):
            send(st_own.at[l, 1], st_y.at[l, y], sy_s, sy_r.at[l], y_peer(d))

    def stats_z(l):
        got(st_y.at[l, pl.ds(0, NY - 1)], sy_r.at[l])
        put(st_own.at[l, 2], merged([st_y[l, i] for i in range(NY)]))
        st_z[l, z] = st_own[l, 2]
        for d in Z_ORDER:
            send(st_own.at[l, 2], st_z.at[l, z], sz_s, sz_r.at[l], z_peer(d))

    def stats_end(l):
        got(st_z.at[l, pl.ds(0, NZ - 1)], sz_r.at[l])
        peak, total, hit = merged([st_z[l, i] for i in range(NZ)])
        lse = peak + jnp.log(total)
        lower = lax.broadcasted_iota(jnp.int32, (1, LANES), 1) < 64
        lines = [jnp.where(lower, tx[s, 1:2, :], tx[s + 1, 1:2, :]) for s in (0, 2)]
        weights = jnp.concatenate(lines, axis=0)
        st_end[l, 0:2, :] = weights * jnp.exp(st_own[l, 0, 0:2, :] - lse)
        st_end[l, 2:4, :] = weights * (jnp.exp(hit - lse) - 1.0)
        st_end[l, 4:6, :] = lse
        st_end[l, 6:8, :] = weights
        mine = (lax.broadcasted_iota(jnp.int32, (2, LANES), 1) // 64 == x % 2) & (
            lax.broadcasted_iota(jnp.int32, (2, LANES), 0) == x // 2
        )
        gap = jnp.where(mine, lse - hit, 0.0)
        return jnp.sum(gap[0:1] + gap[1:2], axis=1, keepdims=True)

    small = lax.broadcasted_iota(jnp.int32, (NZ, LANES), 1)
    small_sub = lax.broadcasted_iota(jnp.int32, (NZ, LANES), 0)

    def own_column(lines, py):
        parts = []
        for s in range(NX):
            here = small == small_sub + (s % 2) * 64 + py * GROUP + c * NZ
            line = lines[s // 2 : s // 2 + 1]
            parts.append(jnp.sum(jnp.where(here, line, 0.0), axis=1, keepdims=True))
        return jnp.concatenate(parts, axis=0)

    def product(l, d):
        py = from_y(d)
        got(u.at[l, py, pl.ds(0, NX - 1)], ux_r.at[l, d])
        out = jnp.dot(u[l, py].reshape(CHUNK, WIDTH), wt[...], preferred_element_type=F32)
        for s in range(NX):
            for cc in range(2):
                at0 = s * GROUP + cc * NZ
                both[l, cc, py, s * NZ : (s + 1) * NZ, :] = out[at0 : at0 + NZ]
        core_out[l, py] = both[l, oc, py].astype(BF16)
        send(core_out.at[l, py], core_in.at[l, py], gc_s, gc_r.at[l, d], core_peer)

    def chip_sum(l, py):
        peak = st_own[l, 1, 0:2, :]
        mine = own_column(jnp.exp(st_own[l, 0, 0:2, :] - peak), py)
        other = own_column(jnp.exp(st_core[l, 0:2, :] - peak), py)
        return mine * both[l, c, py] + other * core_in[l, py].astype(F32)

    def hidden_y(l, d):
        py = from_y(d)
        got(core_in.at[l, py], gc_r.at[l, d])
        y_out[l, d - 1] = chip_sum(l, py).astype(BF16)
        send(y_out.at[l, d - 1], y_in.at[l, d - 1], gy_s, gy_r.at[l], y_peer(NY - d))

    def as_tiles(acc, out):
        for j in range(SUB):
            f[pl.ds(j, NX * NZ, stride=SUB), :] = acc[:, j * LANES : (j + 1) * LANES]
        out[...] = f[: NX * NZ * SUB, :].reshape(NX, NZ, SUB, LANES).astype(BF16)

    def hidden_z(l):
        got(core_in.at[l, y], gc_r.at[l, 0])
        got(y_in.at[l], gy_r.at[l])
        peak = st_own[l, 2, 0:2, :]
        acc = own_column(jnp.exp(st_y[l, y, 0:2, :] - peak), y) * chip_sum(l, y)
        for d in range(1, NY):
            factor = own_column(jnp.exp(st_y[l, (y + d) % NY, 0:2, :] - peak), y)
            acc = acc + factor * y_in[l, d - 1].astype(F32)
        as_tiles(acc, z_out.at[l])
        z_in[l, z] = z_out[l, :, z]
        for d in Z_ORDER:
            send(z_out.at[l, :, (z + d) % NZ], z_in.at[l, z], gz_s, gz_r.at[l], z_peer(d))

    def hidden_x(l):
        got(z_in.at[l, pl.ds(0, NZ - 1)], gz_r.at[l])
        line_at = lax.broadcasted_iota(jnp.int32, (1, LANES), 1)

        def of_row(lines, s):
            here = line_at == (s % 2) * 64 + y * GROUP + c * NZ + z
            return jnp.sum(jnp.where(here, lines[s // 2 : s // 2 + 1], 0.0), axis=1, keepdims=True)

        entries = st_end[l, 2:4, :]
        sums = [jnp.zeros((SUB, LANES), F32)] * NX
        for i in range(NZ):
            lines = st_end[l, 6:8, :] * jnp.exp(st_z[l, i, 0:2, :] - st_end[l, 4:6, :])
            for s in range(NX):
                sums[s] = sums[s] + of_row(lines, s) * z_in[l, i, s].astype(F32)
        for s in range(NX):
            at_target = tz_in[l, 0, s].astype(F32)
            for i in range(1, NZ):
                at_target = at_target + tz_in[l, i, s].astype(F32)
            x_out[s, l] = (sums[s] + of_row(entries, s) * at_target).astype(BF16)

    def target_core(l):
        send(hot_w.at[l, oc], tcore_in.at[l], tc_s, tc_r.at[l], core_peer)

    def target_y(l):
        got(tcore_in.at[l], tc_r.at[l])
        for d in (1, 3, 2):
            py = (y + d) % NY
            ty_out[l, d - 1] = (hot_w[l, c, py].astype(F32) + tcore_in[l, py].astype(F32)).astype(BF16)
            send(ty_out.at[l, d - 1], ty_in.at[l, d - 1], ty_s, ty_r.at[l], y_peer(d))

    def target_z(l):
        got(ty_in.at[l], ty_r.at[l])
        acc = hot_w[l, c, y].astype(F32) + tcore_in[l, y].astype(F32)
        for d in range(1, NY):
            acc = acc + ty_in[l, d - 1].astype(F32)
        as_tiles(acc, tz_out.at[l])
        tz_in[l, z] = tz_out[l, :, z]
        for d in Z_ORDER:
            send(tz_out.at[l, :, (z + d) % NZ], tz_in.at[l, z], tz_s, tz_r.at[l], z_peer(d))

    def target_end(l):
        got(tz_in.at[l, pl.ds(0, NZ - 1)], tz_r.at[l])

    def gradient(l):
        for py in range(NY):
            for s in range(NX):
                factor = as_column(st_end[l, 0:2, :], s, py)
                entry = as_column(st_end[l, 2:4, :], s, py)
                here = columns == target_column(s, l, py)
                value = jnp.where(here, entry, u[l, py, s].astype(F32) * factor)
                grad[rows_of(l, py, s, GROUP), :] = value.astype(BF16)

    gathered_z(0)
    logits_part(0, 0)
    gathered_z(1)
    logits_part(1, 0)
    target_core(0)
    gathered_y(0, 1)
    gathered_y(0, 3)
    logits_relay(0, 0)
    logits_part(0, 1)
    logits_relay(1, 0)
    logits_part(0, 3)
    gathered_y(0, 2)
    target_core(1)
    softmax_part(0, 0)
    raised_out(0, 0)
    logits_part(0, 2)
    target_y(0)
    gathered_y(1, 1)
    logits_relay(0, 1)
    gathered_y(1, 3)
    logits_part(1, 1)
    logits_relay(0, 3)
    softmax_part(1, 0)
    logits_part(1, 3)
    logits_relay(0, 2)
    gathered_y(1, 2)
    target_y(1)
    softmax_part(0, 1)
    raised_out(0, 1)
    logits_part(1, 2)
    softmax_part(0, 3)
    raised_out(0, 3)
    logits_relay(1, 1)
    logits_relay(1, 3)
    product(0, 0)
    softmax_part(0, 2)
    stats_x(0)
    logits_relay(1, 2)
    raised_out(0, 2)
    product(0, 1)
    product(0, 3)
    softmax_part(1, 1)
    raised_out(1, 1)
    stats_core(0)
    softmax_part(1, 3)
    raised_out(1, 3)
    stats_y(0)
    hidden_y(0, 1)
    hidden_y(0, 3)
    softmax_part(1, 2)
    stats_x(1)
    raised_out(1, 2)
    raised_out(1, 0)
    target_z(0)
    target_z(1)
    product(0, 2)
    product(1, 1)
    hidden_y(0, 2)
    stats_core(1)
    product(1, 3)
    stats_z(0)
    stats_y(1)
    hidden_y(1, 1)
    product(1, 2)
    hidden_y(1, 3)
    hidden_y(1, 2)
    stats_z(1)
    loss0 = stats_end(0)
    hidden_z(0)
    product(1, 0)
    hidden_z(1)
    loss1 = stats_end(1)
    gradient(0)
    gradient(1)
    loss[...] = (loss0 + loss1) * (1.0 / 128.0)

    def head_tile(n, _):
        rows = pl.ds(pl.multiple_of(n * 512, 512), 512)
        out = lax.dot_general(
            h[:, rows], grad[...], (((0,), (0,)), ((), ())), preferred_element_type=F32
        )
        head[rows, :] = out.astype(BF16)
        return 0

    lax.fori_loop(0, FEAT // 512, head_tile, 0)
    target_end(0)
    target_end(1)
    hidden_x(0)
    hidden_x(1)
    x_in[x] = x_out[x]
    for d in range(1, NX):
        send(x_out.at[(x + d) % NX], x_in.at[x], gx_s, gx_r, x_peer(d))
    got(x_in.at[pl.ds(0, NX - 1)], gx_r)
    hs32[...] = x_in[...].astype(F32)
    for xx in range(NX):
        for k in range(SUB):
            at0 = xx * FEAT + k * LANES
            ghid[0, :, at0 : at0 + LANES] = hs32[xx, :, k, :].astype(BF16)

    got(hs.at[pl.ds(0, 3)], hx_s)
    got(tx.at[pl.ds(0, 3)], tx_s)
    got(g.at[:, 0, :, 0, pl.ds(0, NZ - 1)], hz_s)
    got(g.at[:, pl.ds(0, NY - 1), :, 0], hy_s)
    got(g.at[:, :, :, 0], hc_s)
    got(relay, rl_s)
    got(final, fn_s)
    got(u.at[:, :, pl.ds(0, NX - 1)], ux_s)
    got(st_core, sc_s)
    got(st_y.at[:, pl.ds(0, NY - 1)], sy_s)
    got(st_z.at[:, pl.ds(0, NZ - 1)], sz_s)
    got(st_raw.at[:, pl.ds(0, NX - 1)], sx_s)
    got(tcore_in, tc_s)
    got(ty_in, ty_s)
    got(tz_in.at[:, pl.ds(0, NZ - 1)], tz_s)
    got(core_in, gc_s)
    got(y_in, gy_s)
    got(z_in.at[:, pl.ds(0, NZ - 1)], gz_s)
    got(x_in.at[pl.ds(0, NX - 1)], gx_s)


def on_device(hidden, out_head, targets, scale_index):
    vmem = pltpu.VMEM
    dma = pltpu.SemaphoreType.DMA
    scratch = [
        vmem((1, 2, NX * FEAT), BF16),
        vmem((1, LANES), jnp.int32),
        vmem((FEAT, WIDTH), BF16),
        vmem((WIDTH, FEAT), BF16),
        vmem((NX, 2, SUB, LANES), F32),
        vmem((NX, 2, SUB, LANES), BF16),
        vmem((2, NY, NX, 2, NZ, SUB, LANES), BF16),
        vmem((CHUNK * SUB, LANES), F32),
        vmem((2 * PART, FEAT), BF16),
        vmem((2 * NY, NX, GROUP, WIDTH), F32),
        vmem((2 * NY, 2, GROUP, HALF), F32),
        vmem((2 * NY, 2, GROUP, WIDTH), F32),
        vmem((2, NY, NX, GROUP, WIDTH), BF16),
        vmem((2 * PART, WIDTH), BF16),
        vmem((PART, WIDTH), BF16),
        vmem((2, 2, NY, NX * NZ, FEAT), BF16),
        vmem((NX, 8, LANES), F32),
        vmem((2, NX, 8, LANES), F32),
        vmem((2, 3, 8, LANES), F32),
        vmem((2, 8, LANES), F32),
        vmem((2, NY, 8, LANES), F32),
        vmem((2, NZ, 8, LANES), F32),
        vmem((2, 8, LANES), F32),
        vmem((2, NY, NX * NZ, FEAT), BF16),
        vmem((2, NY, NX * NZ, FEAT), BF16),
        vmem((2, 2, NY, NX * NZ, FEAT), F32),
        vmem((2, NY - 1, NX * NZ, FEAT), BF16),
        vmem((2, NY - 1, NX * NZ, FEAT), BF16),
        vmem((2, NX, NZ, SUB, LANES), BF16),
        vmem((2, NZ, NX, SUB, LANES), BF16),
        vmem((NX, 2, SUB, LANES), BF16),
        vmem((NX, 2, SUB, LANES), BF16),
        vmem((2, NY, NX * NZ, FEAT), BF16),
        vmem((2, NY - 1, NX * NZ, FEAT), BF16),
        vmem((2, NY - 1, NX * NZ, FEAT), BF16),
        vmem((2, NX, NZ, SUB, LANES), BF16),
        vmem((2, NZ, NX, SUB, LANES), BF16),
        dma, dma, dma, dma, dma, dma((2,)), dma((2, 3)), dma((2, 4)), dma((8, 2)), dma((8, 2)), dma((2, 4)),
        dma((2,)), dma((2,)), dma((2,)), dma((2,)), dma((2, 4)), dma((2,)), dma((2,)), dma,
    ] + [dma] * 16 + [dma((2,))] * 3 + [dma] * 3
    stay = functools.partial(pltpu.with_memory_space_constraint, memory_space=pltpu.HBM)
    in_hbm = pl.BlockSpec(memory_space=pltpu.HBM)
    in_vmem = pl.BlockSpec(memory_space=pltpu.VMEM)
    head, ghid, loss = pl.pallas_call(
        kernel,
        out_shape=(
            jax.ShapeDtypeStruct((FEAT, WIDTH), BF16),
            jax.ShapeDtypeStruct(hidden.shape, BF16),
            jax.ShapeDtypeStruct((1, 1), F32),
        ),
        in_specs=[
            in_hbm,
            in_hbm,
            in_hbm,
            pl.BlockSpec(memory_space=pltpu.SMEM),
        ],
        out_specs=(in_vmem, in_vmem, in_vmem),
        scratch_shapes=scratch,
        compiler_params=pltpu.CompilerParams(
            collective_id=0, has_side_effects=True, vmem_limit_bytes=VMEM_MIB * 2**20
        ),
    )(stay(hidden), out_head, stay(targets), scale_index)
    return head, ghid, loss.reshape(1)


def solution(mesh):
    in_specs = (
        P("section", "vocab", None),
        P("section", "vocab"),
        P("section", None),
        P("section"),
    )
    out_specs = (P("section", "vocab"), P("section", "vocab", None), P("section"))
    return jax.shard_map(
        on_device, mesh=mesh, in_specs=in_specs, out_specs=out_specs, check_vma=False
    )
```

```python
import functools

import jax
import jax.numpy as jnp
from jax import lax
from jax.experimental import pallas as pl
from jax.experimental.pallas import tpu as pltpu
from jax.sharding import PartitionSpec as P

MESH = pl.DeviceIdType.MESH
F32 = jnp.float32
BF16 = jnp.bfloat16

NX, NZ, NY = 4, 8, 4
LANES = 128
SUB = 16
FEAT = SUB * LANES
WIDTH = 1024
HALF = WIDTH // 2
GROUP = 2 * NZ
CHUNK = NX * GROUP
PART = NY * CHUNK
VMEM_MIB = 46
Z_ORDER = (4, 3, 5, 2, 6, 1, 7)


def kernel(
    hid_hbm, w_hbm, tgt_hbm, scale, head, ghid, loss,
    hid, tgt, w, wt, hs32, hs, g, f, h, part, relay, final, u, grad, hot, hot_w,
    tx, st_raw, st_own, st_core, st_y, st_z, st_end,
    core_out, core_in, both, y_out, y_in, z_out, z_in, x_out, x_in,
    tcore_in, ty_out, ty_in, tz_out, tz_in,
    hid_sem, tgt_sem, w_sem, hx_r, tx_r, hz_r, hy_r, hc_r, rl_r, fn_r, ux_r,
    sc_r, sy_r, sz_r, sx_r, gc_r, gy_r, gz_r, gx_r,
    hx_s, tx_s, hz_s, hy_s, hc_s, rl_s, fn_s, ux_s,
    st_s, gc_s, gy_s, gz_s, gx_s, tc_r, ty_r, tz_r, tc_s, ty_s, tz_s,
):
    x = lax.axis_index("section")
    v = lax.axis_index("vocab")
    z, y, c = v // 8, (v // 2) % 4, v % 2
    oc = 1 - c

    def at(px, pz, py, pc):
        return (px, (pz * NY + py) * 2 + pc)

    def x_peer(d):
        return at((x + d) % NX, z, y, c)

    def y_peer(d):
        return at(x, z, (y + d) % NY, c)

    def z_peer(d):
        return at(x, (z + d) % NZ, y, c)

    core_peer = at(x, z, y, oc)

    def send(src, dst, s_sem, r_sem, peer):
        pltpu.make_async_remote_copy(
            src_ref=src, dst_ref=dst, send_sem=s_sem, recv_sem=r_sem,
            device_id=peer, device_id_type=MESH,
        ).start()

    def got(ref, sem):
        pltpu.make_async_copy(ref, ref, sem).wait()

    hid_copy = pltpu.make_async_copy(hid_hbm, hid, hid_sem)
    hid_copy.start()
    tgt_copy = pltpu.make_async_copy(tgt_hbm, tgt, tgt_sem)
    tgt_copy.start()
    barrier = pltpu.get_barrier_semaphore()
    peers = (
        [x_peer(d) for d in range(1, NX)]
        + [core_peer]
        + [y_peer(d) for d in range(1, NY)]
        + [z_peer(d) for d in range(1, NZ)]
    )
    for peer in peers:
        pl.semaphore_signal(barrier, inc=1, device_id=peer, device_id_type=MESH)

    w_copy = pltpu.make_async_copy(w_hbm, w, w_sem)
    w_copy.start()

    hid_copy.wait()
    own = hid[0].astype(F32)
    for xx in range(NX):
        for k in range(SUB):
            at0 = xx * FEAT + k * LANES
            hs32[xx, :, k, :] = own[:, at0 : at0 + LANES]
    hs[...] = hs32[...].astype(BF16)

    tgt_copy.wait()
    place = lax.broadcasted_iota(jnp.int32, (128, 128), 0)
    row = lax.broadcasted_iota(jnp.int32, (128, 128), 1)
    pl_l, pl_y, pl_c, pl_z = place // 64, (place // 16) % 4, (place // 8) % 2, place % 8
    match = row == pl_z * 16 + pl_y * 4 + pl_c * 2 + pl_l
    tcol_all = jnp.sum(
        jnp.where(match, tgt[...].astype(F32), 0.0), axis=1, keepdims=True
    )
    weight = 4.0 * (jnp.full((1, LANES), scale[0], jnp.int32).astype(F32) + 1.0)
    tx[x] = jnp.zeros((8, LANES), F32)
    tx[x, 0:1, :] = jnp.sum(jnp.where(place == row, tcol_all, 0.0), axis=0, keepdims=True)
    tx[x, 1:2, :] = weight
    st_raw[...] = jnp.zeros_like(st_raw)
    st_own[...] = jnp.zeros_like(st_own)

    pl.semaphore_wait(barrier, len(peers))

    for d in range(1, NX):
        send(hs.at[(x + d) % NX], g.at[:, y, x, c, z], hx_s, hx_r, x_peer(d))
    for d in range(1, NX):
        send(tx.at[x], tx.at[x], tx_s, tx_r, x_peer(d))
    for l in range(2):
        g[l, y, x, c, z] = hs[x, l]
    got(hs.at[pl.ds(0, 3)], hx_r)

    for l in range(2):
        for d in Z_ORDER:
            piece = g.at[l, y, :, c, z]
            send(piece, piece, hz_s, hz_r.at[l], z_peer(d))

    columns = v * WIDTH + lax.broadcasted_iota(jnp.int32, (GROUP, WIDTH), 1)
    lane = lax.broadcasted_iota(jnp.int32, (GROUP, LANES), 1)
    sub = lax.broadcasted_iota(jnp.int32, (GROUP, LANES), 0)

    def spot(s, py):
        return lane == sub + (s % 2) * 64 + py * GROUP

    def as_column(lines, s, py):
        line = lines[s // 2 : s // 2 + 1]
        return jnp.sum(jnp.where(spot(s, py), line, 0.0), axis=1, keepdims=True)

    def target_column(s, l, py):
        here = lane == sub + (l * NY + py) * GROUP
        return jnp.sum(jnp.where(here, tx[s, 0:1, :], 0.0), axis=1, keepdims=True).astype(jnp.int32)

    def rows_of(l, py, s=0, count=CHUNK):
        return pl.ds(pl.multiple_of((l * NY + py) * CHUNK + s * GROUP, GROUP), count)

    got(tx.at[pl.ds(0, 3)], tx_r)
    w_copy.wait()

    def turn(n, _):
        rows = pl.ds(pl.multiple_of(n * 512, 512), 512)
        wt[:, rows] = w[rows, :].T
        return 0

    lax.fori_loop(0, FEAT // 512, turn, 0)

    for l in range(2):
        for py in range(NY):
            for s in range(NX):
                here = columns == target_column(s, l, py)
                at0 = py * CHUNK + s * GROUP
                hot[at0 : at0 + GROUP, :] = jnp.where(here, 1.0, 0.0).astype(BF16)
        out = jnp.dot(hot[...], wt[...], preferred_element_type=F32)
        for cc in range(2):
            for py in range(NY):
                for s in range(0, NX, 2):
                    at0 = [py * CHUNK + (s + i) * GROUP + cc * NZ for i in range(2)]
                    pair = jnp.concatenate([out[i : i + NZ] for i in at0], axis=0)
                    hot_w[l, cc, py, s * NZ : (s + 2) * NZ, :] = pair.astype(BF16)

    def from_y(d):
        return (y + NY - d) % NY

    def gathered_z(l):
        got(g.at[l, 0, :, 0, pl.ds(0, NZ - 1)], hz_r.at[l])
        block = g.at[l, y, :, c]
        for d in (1, 3, 2):
            send(block, block, hy_s, hy_r.at[l, d - 1], y_peer(d))
        send(block, block, hc_s, hc_r.at[l, 0], core_peer)

    def gathered_y(l, d):
        block = g.at[l, from_y(d), :, c]
        got(block, hy_r.at[l, d - 1])
        send(block, block, hc_s, hc_r.at[l, d], core_peer)

    def logits_part(l, d):
        py, k = from_y(d), l * NY + d
        got(g.at[l, py, :, oc], hc_r.at[l, d])
        f[...] = g[l, py].reshape(CHUNK * SUB, LANES).astype(F32)
        rows = rows_of(l, py)
        for j in range(SUB):
            h[rows, j * LANES : (j + 1) * LANES] = f[pl.ds(j, CHUNK, stride=SUB), :].astype(BF16)
        out = jnp.dot(h[rows, :], w[...], preferred_element_type=F32)
        part[k] = out.reshape(NX, GROUP, WIDTH)
        far = part.at[k, (x + 2) % NX]
        send(far.at[:, pl.ds(0, HALF)], relay.at[k, 0], rl_s, rl_r.at[k], x_peer(1))
        send(far.at[:, pl.ds(HALF, HALF)], relay.at[k, 1], rl_s, rl_r.at[k], x_peer(3))

    def logits_relay(l, d):
        k = l * NY + d
        right, left = (x + 1) % NX, (x + 3) % NX
        got(relay.at[k], rl_r.at[k])
        part[k, right, :, :HALF] = part[k, right, :, :HALF] + relay[k, 0]
        send(part.at[k, right], final.at[k, 0], fn_s, fn_r.at[k], x_peer(1))
        part[k, left, :, HALF:] = part[k, left, :, HALF:] + relay[k, 1]
        send(part.at[k, left], final.at[k, 1], fn_s, fn_r.at[k], x_peer(3))

    def softmax_part(l, d):
        py, k = from_y(d), l * NY + d
        got(final.at[k], fn_r.at[k])
        logits = part[k, x] + final[k, 0] + final[k, 1]
        peak = jnp.max(logits, axis=1, keepdims=True)
        raised = jnp.exp(logits - peak)
        total = jnp.sum(raised, axis=1, keepdims=True)
        here = columns == target_column(x, l, py)
        hit = jnp.sum(jnp.where(here, logits, 0.0), axis=1, keepdims=True)
        u[l, py, x] = jnp.where(here, 0.0, raised).astype(BF16)
        tile = st_raw[l, x]
        which = lax.broadcasted_iota(jnp.int32, (8, LANES), 0)
        for i, value in enumerate((peak, total, hit)):
            line = jnp.sum(jnp.where(spot(x, py), value, 0.0), axis=0, keepdims=True)
            tile = tile + jnp.where(which == 2 * i + x // 2, line, 0.0)
        st_raw[l, x] = tile

    def raised_out(l, d):
        mine = u.at[l, from_y(d), x]
        for other in (1, 3, 2):
            send(mine, mine, ux_s, ux_r.at[l, d], x_peer(other))

    def merged(parts):
        peak = functools.reduce(jnp.maximum, [p[0:2] for p in parts])
        total = functools.reduce(jnp.add, [p[2:4] * jnp.exp(p[0:2] - peak) for p in parts])
        hit = functools.reduce(jnp.add, [p[4:6] for p in parts])
        return peak, total, hit

    def put(ref, values):
        for i, value in enumerate(values):
            ref[2 * i : 2 * i + 2, :] = value

    def stats_x(l):
        for d in range(1, NX):
            send(st_raw.at[l, x], st_raw.at[l, x], st_s, sx_r.at[l], x_peer(d))

    def stats_core(l):
        got(st_raw.at[l, pl.ds(0, NX - 1)], sx_r.at[l])
        st_own[l, 0] = st_raw[l, 0] + st_raw[l, 1] + st_raw[l, 2] + st_raw[l, 3]
        send(st_own.at[l, 0], st_core.at[l], st_s, sc_r.at[l], core_peer)

    def stats_y(l):
        got(st_core.at[l], sc_r.at[l])
        put(st_own.at[l, 1], merged([st_own[l, 0], st_core[l]]))
        st_y[l, y] = st_own[l, 1]
        for d in range(1, NY):
            send(st_own.at[l, 1], st_y.at[l, y], st_s, sy_r.at[l], y_peer(d))

    def stats_z(l):
        got(st_y.at[l, pl.ds(0, NY - 1)], sy_r.at[l])
        put(st_own.at[l, 2], merged([st_y[l, i] for i in range(NY)]))
        st_z[l, z] = st_own[l, 2]
        for d in Z_ORDER:
            send(st_own.at[l, 2], st_z.at[l, z], st_s, sz_r.at[l], z_peer(d))

    def stats_end(l):
        got(st_z.at[l, pl.ds(0, NZ - 1)], sz_r.at[l])
        peak, total, hit = merged([st_z[l, i] for i in range(NZ)])
        lse = peak + jnp.log(total)
        lower = lax.broadcasted_iota(jnp.int32, (1, LANES), 1) < 64
        lines = [jnp.where(lower, tx[s, 1:2, :], tx[s + 1, 1:2, :]) for s in (0, 2)]
        weights = jnp.concatenate(lines, axis=0)
        st_end[l, 0:2, :] = weights * jnp.exp(st_own[l, 0, 0:2, :] - lse)
        st_end[l, 2:4, :] = weights * (jnp.exp(hit - lse) - 1.0)
        st_end[l, 4:6, :] = lse
        st_end[l, 6:8, :] = weights
        mine = (lax.broadcasted_iota(jnp.int32, (2, LANES), 1) // 64 == x % 2) & (
            lax.broadcasted_iota(jnp.int32, (2, LANES), 0) == x // 2
        )
        gap = jnp.where(mine, lse - hit, 0.0)
        return jnp.sum(gap[0:1] + gap[1:2], axis=1, keepdims=True)

    small = lax.broadcasted_iota(jnp.int32, (NZ, LANES), 1)
    small_sub = lax.broadcasted_iota(jnp.int32, (NZ, LANES), 0)

    def own_column(lines, py):
        parts = []
        for s in range(NX):
            here = small == small_sub + (s % 2) * 64 + py * GROUP + c * NZ
            line = lines[s // 2 : s // 2 + 1]
            parts.append(jnp.sum(jnp.where(here, line, 0.0), axis=1, keepdims=True))
        return jnp.concatenate(parts, axis=0)

    def product(l, d):
        py = from_y(d)
        got(u.at[l, py, pl.ds(0, NX - 1)], ux_r.at[l, d])
        out = jnp.dot(u[l, py].reshape(CHUNK, WIDTH), wt[...], preferred_element_type=F32)
        for s in range(NX):
            for cc in range(2):
                at0 = s * GROUP + cc * NZ
                both[l, cc, py, s * NZ : (s + 1) * NZ, :] = out[at0 : at0 + NZ]
        core_out[l, py] = both[l, oc, py].astype(BF16)
        send(core_out.at[l, py], core_in.at[l, py], gc_s, gc_r.at[l, d], core_peer)

    def chip_sum(l, py):
        peak = st_own[l, 1, 0:2, :]
        mine = own_column(jnp.exp(st_own[l, 0, 0:2, :] - peak), py)
        other = own_column(jnp.exp(st_core[l, 0:2, :] - peak), py)
        return mine * both[l, c, py] + other * core_in[l, py].astype(F32)

    def hidden_y(l, d):
        py = from_y(d)
        got(core_in.at[l, py], gc_r.at[l, d])
        y_out[l, d - 1] = chip_sum(l, py).astype(BF16)
        send(y_out.at[l, d - 1], y_in.at[l, d - 1], gy_s, gy_r.at[l], y_peer(NY - d))

    def as_tiles(acc, out):
        for j in range(SUB):
            f[pl.ds(j, NX * NZ, stride=SUB), :] = acc[:, j * LANES : (j + 1) * LANES]
        out[...] = f[: NX * NZ * SUB, :].reshape(NX, NZ, SUB, LANES).astype(BF16)

    def hidden_z(l):
        got(core_in.at[l, y], gc_r.at[l, 0])
        got(y_in.at[l], gy_r.at[l])
        peak = st_own[l, 2, 0:2, :]
        acc = own_column(jnp.exp(st_y[l, y, 0:2, :] - peak), y) * chip_sum(l, y)
        for d in range(1, NY):
            factor = own_column(jnp.exp(st_y[l, (y + d) % NY, 0:2, :] - peak), y)
            acc = acc + factor * y_in[l, d - 1].astype(F32)
        as_tiles(acc, z_out.at[l])
        z_in[l, z] = z_out[l, :, z]
        for d in Z_ORDER:
            send(z_out.at[l, :, (z + d) % NZ], z_in.at[l, z], gz_s, gz_r.at[l], z_peer(d))

    def hidden_x(l):
        got(z_in.at[l, pl.ds(0, NZ - 1)], gz_r.at[l])
        line_at = lax.broadcasted_iota(jnp.int32, (1, LANES), 1)

        def of_row(lines, s):
            here = line_at == (s % 2) * 64 + y * GROUP + c * NZ + z
            return jnp.sum(jnp.where(here, lines[s // 2 : s // 2 + 1], 0.0), axis=1, keepdims=True)

        entries = st_end[l, 2:4, :]
        sums = [jnp.zeros((SUB, LANES), F32)] * NX
        for i in range(NZ):
            lines = st_end[l, 6:8, :] * jnp.exp(st_z[l, i, 0:2, :] - st_end[l, 4:6, :])
            for s in range(NX):
                sums[s] = sums[s] + of_row(lines, s) * z_in[l, i, s].astype(F32)
        for s in range(NX):
            at_target = tz_in[l, 0, s].astype(F32)
            for i in range(1, NZ):
                at_target = at_target + tz_in[l, i, s].astype(F32)
            x_out[s, l] = (sums[s] + of_row(entries, s) * at_target).astype(BF16)

    def target_core(l):
        send(hot_w.at[l, oc], tcore_in.at[l], tc_s, tc_r.at[l], core_peer)

    def target_y(l):
        got(tcore_in.at[l], tc_r.at[l])
        for d in (1, 3, 2):
            py = (y + d) % NY
            ty_out[l, d - 1] = (hot_w[l, c, py].astype(F32) + tcore_in[l, py].astype(F32)).astype(BF16)
            send(ty_out.at[l, d - 1], ty_in.at[l, d - 1], ty_s, ty_r.at[l], y_peer(d))

    def target_z(l):
        got(ty_in.at[l], ty_r.at[l])
        acc = hot_w[l, c, y].astype(F32) + tcore_in[l, y].astype(F32)
        for d in range(1, NY):
            acc = acc + ty_in[l, d - 1].astype(F32)
        as_tiles(acc, tz_out.at[l])
        tz_in[l, z] = tz_out[l, :, z]
        for d in Z_ORDER:
            send(tz_out.at[l, :, (z + d) % NZ], tz_in.at[l, z], tz_s, tz_r.at[l], z_peer(d))

    def target_end(l):
        got(tz_in.at[l, pl.ds(0, NZ - 1)], tz_r.at[l])

    def gradient(l):
        for py in range(NY):
            for s in range(NX):
                factor = as_column(st_end[l, 0:2, :], s, py)
                entry = as_column(st_end[l, 2:4, :], s, py)
                here = columns == target_column(s, l, py)
                value = jnp.where(here, entry, u[l, py, s].astype(F32) * factor)
                grad[rows_of(l, py, s, GROUP), :] = value.astype(BF16)

    gathered_z(0)
    logits_part(0, 0)
    gathered_z(1)
    logits_part(1, 0)
    target_core(0)
    gathered_y(0, 1)
    gathered_y(0, 3)
    logits_relay(0, 0)
    logits_part(0, 1)
    logits_relay(1, 0)
    logits_part(0, 3)
    gathered_y(0, 2)
    target_core(1)
    softmax_part(0, 0)
    raised_out(0, 0)
    logits_part(0, 2)
    target_y(0)
    gathered_y(1, 1)
    logits_relay(0, 1)
    gathered_y(1, 3)
    logits_part(1, 1)
    logits_relay(0, 3)
    softmax_part(1, 0)
    logits_part(1, 3)
    logits_relay(0, 2)
    gathered_y(1, 2)
    target_y(1)
    softmax_part(0, 1)
    raised_out(0, 1)
    logits_part(1, 2)
    softmax_part(0, 3)
    raised_out(0, 3)
    logits_relay(1, 1)
    logits_relay(1, 3)
    product(0, 0)
    softmax_part(0, 2)
    stats_x(0)
    logits_relay(1, 2)
    raised_out(0, 2)
    product(0, 1)
    product(0, 3)
    softmax_part(1, 1)
    raised_out(1, 1)
    stats_core(0)
    softmax_part(1, 3)
    raised_out(1, 3)
    stats_y(0)
    hidden_y(0, 1)
    hidden_y(0, 3)
    softmax_part(1, 2)
    stats_x(1)
    raised_out(1, 2)
    raised_out(1, 0)
    target_z(0)
    target_z(1)
    product(0, 2)
    product(1, 1)
    hidden_y(0, 2)
    stats_core(1)
    product(1, 3)
    stats_z(0)
    stats_y(1)
    hidden_y(1, 1)
    product(1, 2)
    hidden_y(1, 3)
    hidden_y(1, 2)
    stats_z(1)
    loss0 = stats_end(0)
    hidden_z(0)
    product(1, 0)
    hidden_z(1)
    loss1 = stats_end(1)
    gradient(0)
    gradient(1)
    loss[...] = (loss0 + loss1) * (1.0 / 128.0)

    def head_tile(n, _):
        rows = pl.ds(pl.multiple_of(n * 512, 512), 512)
        out = lax.dot_general(
            h[:, rows], grad[...], (((0,), (0,)), ((), ())), preferred_element_type=F32
        )
        head[rows, :] = out.astype(BF16)
        return 0

    lax.fori_loop(0, FEAT // 512, head_tile, 0)
    target_end(0)
    target_end(1)
    hidden_x(0)
    hidden_x(1)
    x_in[x] = x_out[x]
    for d in range(1, NX):
        send(x_out.at[(x + d) % NX], x_in.at[x], gx_s, gx_r, x_peer(d))
    got(x_in.at[pl.ds(0, NX - 1)], gx_r)
    hs32[...] = x_in[...].astype(F32)
    for xx in range(NX):
        for k in range(SUB):
            at0 = xx * FEAT + k * LANES
            ghid[0, :, at0 : at0 + LANES] = hs32[xx, :, k, :].astype(BF16)

    got(hs.at[pl.ds(0, 3)], hx_s)
    got(tx.at[pl.ds(0, 3)], tx_s)
    got(g.at[:, 0, :, 0, pl.ds(0, NZ - 1)], hz_s)
    got(g.at[:, pl.ds(0, NY - 1), :, 0], hy_s)
    got(g.at[:, :, :, 0], hc_s)
    got(relay, rl_s)
    got(final, fn_s)
    got(u.at[:, :, pl.ds(0, NX - 1)], ux_s)
    got(f.at[pl.ds(0, 28 * 8)], st_s)
    got(tcore_in, tc_s)
    got(ty_in, ty_s)
    got(tz_in.at[:, pl.ds(0, NZ - 1)], tz_s)
    got(core_in, gc_s)
    got(y_in, gy_s)
    got(z_in.at[:, pl.ds(0, NZ - 1)], gz_s)
    got(x_in.at[pl.ds(0, NX - 1)], gx_s)


def on_device(hidden, out_head, targets, scale_index):
    vmem = pltpu.VMEM
    dma = pltpu.SemaphoreType.DMA
    scratch = [
        vmem((1, 2, NX * FEAT), BF16),
        vmem((1, LANES), jnp.int32),
        vmem((FEAT, WIDTH), BF16),
        vmem((WIDTH, FEAT), BF16),
        vmem((NX, 2, SUB, LANES), F32),
        vmem((NX, 2, SUB, LANES), BF16),
        vmem((2, NY, NX, 2, NZ, SUB, LANES), BF16),
        vmem((CHUNK * SUB, LANES), F32),
        vmem((2 * PART, FEAT), BF16),
        vmem((2 * NY, NX, GROUP, WIDTH), F32),
        vmem((2 * NY, 2, GROUP, HALF), F32),
        vmem((2 * NY, 2, GROUP, WIDTH), F32),
        vmem((2, NY, NX, GROUP, WIDTH), BF16),
        vmem((2 * PART, WIDTH), BF16),
        vmem((PART, WIDTH), BF16),
        vmem((2, 2, NY, NX * NZ, FEAT), BF16),
        vmem((NX, 8, LANES), F32),
        vmem((2, NX, 8, LANES), F32),
        vmem((2, 3, 8, LANES), F32),
        vmem((2, 8, LANES), F32),
        vmem((2, NY, 8, LANES), F32),
        vmem((2, NZ, 8, LANES), F32),
        vmem((2, 8, LANES), F32),
        vmem((2, NY, NX * NZ, FEAT), BF16),
        vmem((2, NY, NX * NZ, FEAT), BF16),
        vmem((2, 2, NY, NX * NZ, FEAT), F32),
        vmem((2, NY - 1, NX * NZ, FEAT), BF16),
        vmem((2, NY - 1, NX * NZ, FEAT), BF16),
        vmem((2, NX, NZ, SUB, LANES), BF16),
        vmem((2, NZ, NX, SUB, LANES), BF16),
        vmem((NX, 2, SUB, LANES), BF16),
        vmem((NX, 2, SUB, LANES), BF16),
        vmem((2, NY, NX * NZ, FEAT), BF16),
        vmem((2, NY - 1, NX * NZ, FEAT), BF16),
        vmem((2, NY - 1, NX * NZ, FEAT), BF16),
        vmem((2, NX, NZ, SUB, LANES), BF16),
        vmem((2, NZ, NX, SUB, LANES), BF16),
        dma, dma, dma, dma, dma, dma((2,)), dma((2, 3)), dma((2, 4)), dma((8,)), dma((8,)), dma((2, 4)),
        dma((2,)), dma((2,)), dma((2,)), dma((2,)), dma((2, 4)), dma((2,)), dma((2,)), dma,
    ] + [dma] * 13 + [dma((2,))] * 3 + [dma] * 3
    stay = functools.partial(pltpu.with_memory_space_constraint, memory_space=pltpu.HBM)
    in_hbm = pl.BlockSpec(memory_space=pltpu.HBM)
    in_vmem = pl.BlockSpec(memory_space=pltpu.VMEM)
    head, ghid, loss = pl.pallas_call(
        kernel,
        out_shape=(
            jax.ShapeDtypeStruct((FEAT, WIDTH), BF16),
            jax.ShapeDtypeStruct(hidden.shape, BF16),
            jax.ShapeDtypeStruct((1, 1), F32),
        ),
        in_specs=[
            in_hbm,
            in_hbm,
            in_hbm,
            pl.BlockSpec(memory_space=pltpu.SMEM),
        ],
        out_specs=(in_vmem, in_vmem, in_vmem),
        scratch_shapes=scratch,
        compiler_params=pltpu.CompilerParams(
            collective_id=0, has_side_effects=True, vmem_limit_bytes=VMEM_MIB * 2**20
        ),
    )(stay(hidden), out_head, stay(targets), scale_index)
    return head, ghid, loss.reshape(1)


def solution(mesh):
    in_specs = (
        P("section", "vocab", None),
        P("section", "vocab"),
        P("section", None),
        P("section"),
    )
    out_specs = (P("section", "vocab"), P("section", "vocab", None), P("section"))
    return jax.shard_map(
        on_device, mesh=mesh, in_specs=in_specs, out_specs=out_specs, check_vma=False
    )
```
